512 devices in a mesh: role: 4 (over y_lo), dp: 32 (over z, y_hi, core), mp: 4 (over x).
Axes of the slice: x: 4, y: 8 (y_hi: 2, y_lo: 4; y = y_hi * 4 + y_lo), z: 8, core: 2. Of those that a mesh axis runs over, the one named last changes fastest.
Arguments:
- residual_in: bfloat16 [4096, 8, 2048], P(('role', 'dp'), None, 'mp'), may hold values from -6 to 6
- context: bfloat16 [4096, 8, 2048], P(('role', 'dp'), None, 'mp'), may hold values from -6 to 6
- w_out: bfloat16 [2048, 2048], P('dp', 'mp'), may hold values from -0.125 to 0.125
- norm_gain: float32 [2048], P('mp'), may hold values from 0.1 to 1.9
- policy_head: bfloat16 [2048, 43], P('mp'), may hold values from -0.125 to 0.125
- value_head: bfloat16 [2048], P('mp'), may hold values from -0.125 to 0.125
- rewards: bfloat16 [4096, 8], P(('role', 'dp')), may hold values from -12 to 12
- resets: int32 [4096, 8], P(('role', 'dp')), may hold values 0 or 1
- actions: int32 [4096, 8], P(('role', 'dp')), may hold values from 0 to 42
- lengths: int32 [4096], P(('role', 'dp')), may hold values from 1 to 7
- assignment: int32 [4096], P(('role', 'dp')), may hold values from 0 to 31, as said below
Outputs:
- advantages: float32 [4096, 8], P(('role', 'dp'))
- adv_means: float32 [32], P('dp')
- grad_w: float32 [2048, 2048], P('dp', 'mp')
- grad_gain: float32 [2048], P('mp')
- grad_policy: float32 [2048, 43], P('mp')
- grad_value: float32 [2048], P('mp')
The draws below stay inside these ranges and needn't reach their ends.
Inputs may be any that keep to these rules, and one draw needn't show every extreme that they name: `assignment`: each device sends either none or exactly 2 of its environments to each learner index, and each learner index receives exactly 32 environments from the devices of each group. `lengths`: rows 0 to length - 1 of an environment are its trajectory; row length is the observation that bootstraps it.
All inputs are finite; a program needn't handle non-finite values. No bound on the sum of `resets` on one device may be relied on, other than what follows from the above.
Results may differ from the reference program's by a relative error of at most 0.0027.
Values may be sent and summed in bfloat16 or wider, within the bound.
A program may use at most 64 MiB of HBM per device.

```python
import math
import jax
import jax.numpy as jnp
from jax import lax

D = 2048
A = 43
STEPS = 8
ENV_SH = 32
MOST = 2
ENVS = 4096
N_ROLE = 4
N_DP = 32


def shuffle_learners(sub_key):
    return jax.random.permutation(sub_key, N_DP)


def shuffle_envs(sub_key):
    return jax.random.permutation(sub_key, ENV_SH)


def draw_assignment(key, part):
    key = jax.random.fold_in(key, 11)
    key_inner, key_outer, key_offset, key_envs = jax.random.split(key, 4)
    offsets_used = ENV_SH // MOST
    inner_order = jax.vmap(shuffle_learners)(jax.random.split(key_inner, N_ROLE))
    outer_order = jax.vmap(shuffle_learners)(jax.random.split(key_outer, N_ROLE))
    offsets = jax.vmap(shuffle_learners)(jax.random.split(key_offset, N_ROLE))[:, :offsets_used]
    env_order = jax.vmap(shuffle_envs)(jax.random.split(key_envs, N_ROLE * N_DP)).reshape(N_ROLE, N_DP, ENV_SH)
    group_slot = env_order // MOST
    offsets_wide = jnp.broadcast_to(offsets[:, None, :], (N_ROLE, N_DP, offsets_used))
    chosen_offset = jnp.take_along_axis(offsets_wide, group_slot, axis=2)
    spot = (inner_order[:, :, None] + chosen_offset) % N_DP
    outer_wide = jnp.broadcast_to(outer_order[:, None, :], (N_ROLE, N_DP, N_DP))
    learner = jnp.take_along_axis(outer_wide, spot, axis=2)
    return learner.reshape(-1).astype(jnp.int32)


def draw_rewards(key, part):
    key = jax.random.fold_in(key, 7)
    key_env, key_step, key_base = jax.random.split(key, 3)
    env_scale = jnp.exp(jax.random.uniform(key_env, (ENVS, 1), jnp.float32, math.log(0.3), math.log(3.0)))
    step_scale = jnp.exp(jax.random.uniform(key_step, (1, STEPS), jnp.float32, math.log(0.5), math.log(2.0)))
    base = jnp.clip(jax.random.normal(key_base, (ENVS, STEPS), jnp.float32), -2.0, 2.0)
    return (env_scale * step_scale * base).astype(jnp.bfloat16)


def set_ends(values, key, smallest, largest):
    dims = values.shape
    spot = [jax.random.randint(jax.random.fold_in(key, axis), (), 0, dims[axis]) for axis in range(len(dims))]
    values = values.at[tuple(spot)].set(smallest)
    longest = dims.index(max(dims))
    spot[longest] = (spot[longest] + 1) % dims[longest]
    return values.at[tuple(spot)].set(largest)


def steps_of(key, shape, cuts, low, largest):
    factor_of, own = 1.0, jax.random.fold_in(key, 6)
    for dim, blocks in cuts:
        heights = jnp.exp(jax.random.uniform(jax.random.fold_in(own, dim), (blocks,), jnp.float32, low / len(cuts), largest / len(cuts)))
        factor_of = factor_of * jnp.repeat(heights, shape[dim] // blocks).reshape([-1 if axis == dim else 1 for axis in range(len(shape))])
    return factor_of


def gaussian(key, dims, deviation, limit, shards=(), dtype=jnp.bfloat16):
    level = steps_of(key, dims, shards, -0.22, 0.18) if shards else 1.0
    array = jax.random.normal(key, dims, jnp.float32) * deviation * level
    return jnp.minimum(jnp.maximum(array, -limit), limit).astype(dtype)


def setup_inputs(seed: int = 0) -> dict:
    key_of = jax.random.split(jax.random.key(seed), 12)
    return {
        "residual_in": gaussian(key_of[0], (ENVS, STEPS, D), 1.0, 6.0, ((0, 128), (2, 4))),
        "context": gaussian(key_of[1], (ENVS, STEPS, D), 1.0, 6.0, ((0, 128), (2, 4))),
        "w_out": gaussian(key_of[2], (D, D), D ** -0.5, 0.125, ((0, 32), (1, 4))),
        "norm_gain": jnp.clip(1.0 + 0.18 * jax.random.normal(key_of[3], (D,), jnp.float32), 0.1, 1.9),
        "policy_head": gaussian(key_of[4], (D, A), D ** -0.5, 0.125, ((0, 4),)),
        "value_head": gaussian(key_of[5], (D,), D ** -0.5, 0.125, ((0, 4),)),
        "rewards": draw_rewards(jax.random.fold_in(key_of[11], 71), 0),
        "resets": set_ends((jax.random.randint(key_of[7], (ENVS, STEPS), 0, 8) < 1).astype(jnp.int32), jax.random.fold_in(key_of[7], 1), 0, 1),
        "actions": set_ends(jax.random.randint(key_of[8], (ENVS, STEPS), 0, A), jax.random.fold_in(key_of[8], 1), 0, A - 1).astype(jnp.int32),
        "lengths": set_ends(jax.random.randint(key_of[9], (ENVS,), 1, STEPS), jax.random.fold_in(key_of[9], 1), 1, STEPS - 1).astype(jnp.int32),
        "assignment": draw_assignment(jax.random.fold_in(key_of[11], 71), 0),
    }


discount = 0.99
trace_decay = 0.95
value_weight = 0.5
epsilon = 1e-05
highest = lax.Precision.HIGHEST

def advantage_estimate(rewards, resets, values, lengths):
    num_env, num_steps = values.shape
    valid = (jnp.arange(num_steps)[None, :] < lengths[:, None]).astype(jnp.float32)
    next_values = jnp.concatenate([values[:, 1:], jnp.zeros((num_env, 1), jnp.float32)], axis=1)
    carry_on = 1.0 - resets.astype(jnp.float32)
    deltas = rewards.astype(jnp.float32) + discount * carry_on * next_values - values

    def step_back(later, inputs):
        delta_now, keep_now, valid_now = inputs
        current = valid_now * (delta_now + discount * trace_decay * keep_now * later)
        return (current, current)
    final_carry, stacked = lax.scan(step_back, jnp.zeros((num_env,), jnp.float32), (deltas.T, carry_on.T, valid.T), reverse=True)
    return (stacked.T, valid)

def reference(residual_in, context, w_out, norm_gain, policy_head, value_head, rewards, resets, actions, lengths, assignment):
    num_env, num_steps, width = context.shape
    flat_context = context.reshape(num_env * num_steps, width)
    stream = residual_in.reshape(num_env * num_steps, width).astype(jnp.float32) + jnp.dot(flat_context, w_out, preferred_element_type=jnp.float32)
    inverse = lax.rsqrt(lax.optimization_barrier(jnp.sum(stream * stream, axis=1)) / width + epsilon)
    normed = stream * inverse[:, None] * norm_gain
    policy = policy_head.astype(jnp.float32)
    value_vec = value_head.astype(jnp.float32)
    logits = jnp.dot(normed, policy, precision=highest)
    values = jnp.dot(normed, value_vec, precision=highest)
    value_grid = values.reshape(num_env, num_steps)
    advantages, valid = advantage_estimate(rewards, resets, value_grid, lengths)
    returns = advantages + value_grid
    target_hit = (assignment[:, None] == jnp.arange(N_DP)[None, :]).astype(jnp.float32)
    counts = jnp.dot(lengths.astype(jnp.float32), target_hit, precision=highest)
    sums = jnp.dot(lax.optimization_barrier(jnp.sum(advantages, axis=1)), target_hit, precision=highest)
    adv_means = sums / counts
    env_count = jnp.dot(target_hit, counts, precision=highest)
    env_mean = jnp.dot(target_hit, adv_means, precision=highest)
    centered = (advantages - env_mean[:, None]).reshape(-1)
    weight = (valid / env_count[:, None]).reshape(-1)
    log_probs = logits - jnp.log(lax.optimization_barrier(jnp.sum(jnp.exp(logits), axis=1, keepdims=True)))
    chosen = (actions.reshape(-1)[:, None] == jnp.arange(logits.shape[1])[None, :]).astype(jnp.float32)
    grad_logits = (weight * centered)[:, None] * (jnp.exp(log_probs) - chosen)
    grad_values = value_weight * weight * (values - returns.reshape(-1))
    grad_normed = jnp.dot(grad_logits, policy.T, precision=highest) + grad_values[:, None] * value_vec
    grad_policy = jnp.dot(normed.T, grad_logits, precision=highest)
    grad_value = jnp.dot(grad_values, normed, precision=highest)
    grad_gain = lax.optimization_barrier(jnp.sum(grad_normed * stream * inverse[:, None], axis=0))
    inner = lax.optimization_barrier(jnp.sum(grad_normed * norm_gain * stream, axis=1))
    grad_stream = inverse[:, None] * norm_gain * grad_normed - stream * (inverse * inverse * inverse * inner / width)[:, None]
    grad_stream = grad_stream.astype(jnp.bfloat16)
    grad_w = lax.dot_general(flat_context, grad_stream, (((0,), (0,)), ((), ())), preferred_element_type=jnp.float32)
    return (advantages, adv_means, grad_w, grad_gain, grad_policy, grad_value)
```

```python
import jax
import jax.numpy as jnp
from jax import lax
from jax.sharding import PartitionSpec as P

D = 2048


discount = 0.99
trace_decay = 0.95
value_weight = 0.5
epsilon = 1e-05
highest = lax.Precision.HIGHEST


def advantage_estimate(rewards, resets, values, lengths):
    num_env, num_steps = values.shape
    valid = (jnp.arange(num_steps)[None, :] < lengths[:, None]).astype(jnp.float32)
    next_values = jnp.concatenate([values[:, 1:], jnp.zeros((num_env, 1), jnp.float32)], axis=1)
    carry_on = 1.0 - resets.astype(jnp.float32)
    deltas = rewards.astype(jnp.float32) + discount * carry_on * next_values - values

    def step_back(later, inputs):
        delta_now, keep_now, valid_now = inputs
        current = valid_now * (delta_now + discount * trace_decay * keep_now * later)
        return (current, current)

    final_carry, stacked = lax.scan(
        step_back, jnp.zeros((num_env,), jnp.float32), (deltas.T, carry_on.T, valid.T), reverse=True
    )
    return (stacked.T, valid)


def per_device(
    residual_in,
    context,
    w_out,
    norm_gain,
    policy_head,
    value_head,
    rewards,
    resets,
    actions,
    lengths,
    assignment,
):
    num_env, num_steps, width_cols = context.shape
    rows = num_env * num_steps
    learners = lax.axis_size("dp")
    num_actions = policy_head.shape[1]
    weights = lax.all_gather(w_out, "dp", axis=0, tiled=True)
    context_full = lax.all_gather(context, "mp", axis=2, tiled=True).reshape(rows, -1)
    heads = jnp.concatenate([policy_head, value_head[:, None]], axis=1).astype(jnp.float32)
    stream = residual_in.reshape(rows, width_cols).astype(jnp.float32) + jnp.dot(
        context_full, weights, preferred_element_type=jnp.float32
    )
    scaled = stream * norm_gain
    raw, squares = lax.psum(
        (jnp.dot(scaled, heads, precision=highest), jnp.sum(stream * stream, axis=1)), "mp"
    )
    inverse = lax.rsqrt(squares / D + epsilon)
    out = raw * inverse[:, None]
    logits, values = out[:, :num_actions], out[:, num_actions]
    value_grid = values.reshape(num_env, num_steps)
    advantages, valid = advantage_estimate(rewards, resets, value_grid, lengths)
    returns = advantages + value_grid
    target_hit = (assignment[:, None] == jnp.arange(learners)[None, :]).astype(jnp.float32)
    both = jnp.stack([lengths.astype(jnp.float32), jnp.sum(advantages, axis=1)])
    totals = lax.psum(jnp.dot(both, target_hit, precision=highest), ("role", "dp"))
    counts, means = totals[0], totals[1] / totals[0]
    env_count = jnp.dot(target_hit, counts, precision=highest)
    env_mean = jnp.dot(target_hit, means, precision=highest)
    centered = (advantages - env_mean[:, None]).reshape(-1)
    weight = (valid / env_count[:, None]).reshape(-1)
    log_probs = logits - jnp.log(jnp.sum(jnp.exp(logits), axis=1, keepdims=True))
    chosen = (actions.reshape(-1)[:, None] == jnp.arange(num_actions)[None, :]).astype(jnp.float32)
    grad_logits = (weight * centered)[:, None] * (jnp.exp(log_probs) - chosen)
    grad_values = value_weight * weight * (values - returns.reshape(-1))
    grad_out = jnp.concatenate([grad_logits, grad_values[:, None]], axis=1)
    grad_normed = jnp.dot(grad_out, heads.T, precision=highest)
    grad_heads = jnp.dot((scaled * inverse[:, None]).T, grad_out, precision=highest)
    gain_grad = jnp.sum(grad_normed * stream * inverse[:, None], axis=0)
    inner = jnp.sum(grad_out * raw, axis=1)
    grad_stream = (
        inverse[:, None] * norm_gain * grad_normed
        - stream * (inverse * inverse * inverse * inner / D)[:, None]
    ).astype(jnp.bfloat16)
    grad_w = lax.psum_scatter(
        lax.dot_general(
            context_full, grad_stream, (((0,), (0,)), ((), ())), preferred_element_type=jnp.float32
        ),
        "dp",
        scatter_dimension=0,
        tiled=True,
    )
    grad_w = lax.psum(grad_w, "role")
    grad_heads, gain_grad = lax.psum((grad_heads, gain_grad), ("role", "dp"))
    adv_means = lax.dynamic_slice(means, (lax.axis_index("dp"),), (1,))
    return (
        advantages,
        adv_means,
        grad_w,
        gain_grad,
        grad_heads[:, :num_actions],
        grad_heads[:, num_actions],
    )


def solution(mesh):
    placed = (
        P(("role", "dp"), None, "mp"),
        P(("role", "dp"), None, "mp"),
        P("dp", "mp"),
        P("mp"),
        P("mp", None),
        P("mp"),
        P(("role", "dp"), None),
        P(("role", "dp"), None),
        P(("role", "dp"), None),
        P(("role", "dp")),
        P(("role", "dp")),
    )
    return jax.shard_map(
        per_device,
        mesh=mesh,
        in_specs=placed,
        out_specs=(
            P(("role", "dp"), None),
            P("dp"),
            P("dp", "mp"),
            P("mp"),
            P("mp", None),
            P("mp"),
        ),
        check_vma=False,
    )
```

```python
import jax
import jax.numpy as jnp
from jax import lax
from jax.experimental import pallas as pl
from jax.experimental.pallas import tpu as pltpu
from jax.sharding import PartitionSpec as P

D = 2048
A = 43
STEPS = 8
ROWS = 256
COLS = 512
HALF = 256
HP = 64
RAW = 48

discount = 0.99
trace_decay = 0.95
value_weight = 0.5
epsilon = 1e-05

MESH = pl.DeviceIdType.MESH
bf16 = jnp.bfloat16
f32 = jnp.float32
i32 = jnp.int32

NN = (((1,), (0,)), ((), ()))
NT = (((1,), (1,)), ((), ()))
TN = (((0,), (0,)), ((), ()))


def mul(a, b, dims):
    return lax.dot_general(a, b, dims, preferred_element_type=f32)


def parts_of(a, n):
    out = []
    for _ in range(n):
        high = a.astype(bf16)
        out.append(high)
        a = a - high.astype(f32)
    return out


def kernel(
    resid, ctx, w, gain, policy, value, rewards, resets, actions, lengths, assign,
    adv_out, misc_out, gw_out, heads_out,
    ctxbuf, wa, wb, wm, psend, precv, stream_s, gstream,
    rawbuf, l1, l2, lsrc, heads_t, qsrc, q1, q2, q2src, qf,
    pb, ra, rb, sa2, sb2, ra2, rb2, fin,
    s_ctx, r_ctx, s_a1, r_a1, s_a2, r_a2, s_b1, r_b1, s_b2, r_b2,
    s_p, r_p, s_raw, r_raw, s_l1, r_l1, s_l2, r_l2, s_g, r_g,
    s_q1, r_q1, s_q2, r_q2, s_q3, r_q3,
    s_ra, r_ra, s_rb, r_rb, s_ra2, r_ra2, s_rb2, r_rb2, s_f, r_f,
):
    role = lax.axis_index("role")
    dp = lax.axis_index("dp")
    x = lax.axis_index("mp")
    z = dp // 4
    h = (dp // 2) % 2
    c = dp % 2
    y = h * 4 + role
    r = role
    o = 1 - c
    kx = x // 2
    kz = z // 4
    me16 = z * 2 + c

    def dev(dx, dy, dz, core):
        yy = (y + dy) % 8
        return {
            "role": yy % 4,
            "dp": ((z + dz) % 8) * 4 + (yy // 4) * 2 + core,
            "mp": (x + dx) % 4,
        }

    mate = dev(0, 0, 0, o)

    def remote(src, dst, send, recv, device):
        return pltpu.make_async_remote_copy(
            src_ref=src,
            dst_ref=dst,
            send_sem=send,
            recv_sem=recv,
            device_id=device,
            device_id_type=MESH,
        )

    pending = []

    def send(src, dst, ssem, rsem, device):
        copy = remote(src, dst, ssem, rsem, device)
        copy.start()
        pending.append((None, copy))

    def send_chip(src, dst, ssem, rsem, core):
        @pl.when(c == core)
        def _():
            pltpu.make_async_copy(src, dst, rsem).start()

        copy = remote(src, dst, ssem, rsem, mate)

        @pl.when(c != core)
        def _():
            copy.start()

        pending.append((c != core, copy))

    def arrived(dst, rsem):
        pltpu.make_async_copy(dst, dst, rsem).wait()

    barrier = pltpu.get_barrier_semaphore()
    peers = [mate]
    for d in range(1, 4):
        peers += [dev(d, 0, 0, 0), dev(d, 0, 0, 1)]
    for d in range(1, 8):
        peers += [dev(0, 0, d, 0), dev(0, 0, d, 1), dev(0, d, 0, c)]
    for peer in peers:
        pl.semaphore_signal(barrier, inc=1, device_id=peer, device_id_type=MESH)
    pl.semaphore_wait(barrier, len(peers))

    slot = (x % 2) * 2 + c
    for d in (2, 1, 3):
        send(ctx, ctxbuf.at[slot], s_ctx.at[d], r_ctx.at[slot], dev(d, 0, 0, kx))
    send_chip(ctx, ctxbuf.at[slot], s_ctx.at[0], r_ctx.at[slot], kx)
    zs = z % 4
    quarter = w.at[pl.ds(pl.multiple_of(r * 16, 16), 16), pl.ds(0, HALF)]
    second = w.at[:, pl.ds(HALF, HALF)]
    mirror = {"role": (7 - y) % 4, "dp": z * 4 + (1 - h) * 2 + c, "mp": x}
    send(second, wm, s_b1.at[0], r_b1.at[0], mirror)
    for d in (4, 3, 5, 2, 6, 1, 7):
        send(quarter, wa.at[zs, h, c, r], s_a1.at[d], r_a1.at[zs * 2 + c], dev(0, 0, d, kz))
    send_chip(quarter, wa.at[zs, h, c, r], s_a1.at[0], r_a1.at[zs * 2 + c], kz)
    bslot = (zs * 2 + h) * 2 + c
    for d in (4, 3, 5, 2, 6, 1, 7):
        send(second, wb.at[bslot], s_b2.at[d], r_b2.at[bslot], dev(0, 0, d, kz))
    send_chip(second, wb.at[bslot], s_b2.at[0], r_b2.at[bslot], kz)

    lane8 = lax.broadcasted_iota(i32, (8, ROWS), 1)
    sub8 = lax.broadcasted_iota(i32, (8, ROWS), 0)
    step = lane8 % STEPS
    spread = (step == sub8).astype(f32).astype(bf16)
    lane32 = lax.broadcasted_iota(i32, (32, ROWS), 1)
    sub32 = lax.broadcasted_iota(i32, (32, ROWS), 0)
    env = lane32 // STEPS == sub32
    env_b = env.astype(f32).astype(bf16)

    def to_row(grid):
        wide = jnp.where(env, mul(grid.astype(f32).astype(bf16), spread, NN), 0.0)
        return jnp.broadcast_to(jnp.sum(wide, axis=0, keepdims=True), (8, ROWS))

    def env_row(vector):
        return mul(jnp.broadcast_to(vector.astype(f32), (8, 32)).astype(bf16), env_b, NN)

    reward = to_row(rewards[...])
    keep = 1.0 - to_row(resets[...])
    action = to_row(actions[...])
    length = env_row(lengths[...])
    learner = env_row(assign[...])
    valid = (step.astype(f32) < length).astype(f32)
    learner_hit = jnp.broadcast_to(learner[0:1], (32, ROWS)) == sub32.astype(f32)
    pick = (
        lax.broadcasted_iota(i32, (HP, A), 0) == lax.broadcasted_iota(i32, (HP, A), 1)
    ).astype(f32).astype(bf16)
    head_rows = lax.broadcasted_iota(i32, (HP, COLS), 0)
    heads_t[...] = jnp.where(
        head_rows == A,
        jnp.broadcast_to(value[...].astype(f32), (HP, COLS)),
        mul(pick, policy[...], NT),
    ).astype(bf16)

    arrived(wm, r_b1.at[0])
    cslot = (zs * 2 + 1 - h) * 2 + c
    for d in (4, 3, 5, 2, 6, 1, 7):
        send(wm, wb.at[cslot], s_b2.at[8 + d], r_b2.at[cslot], dev(0, 0, d, kz))
    send_chip(wm, wb.at[cslot], s_b2.at[8], r_b2.at[cslot], kz)
    for s in range(4):
        for core in range(2):
            arrived(wa.at[s, h, core, r], r_a1.at[s * 2 + core])
    mine = wa.at[:, h, :, r]
    for d in (4, 3, 5, 2, 6, 1, 7):
        send(mine, mine, s_a2.at[d], r_a2.at[y], dev(0, d, 0, c))
    for s in range(4):
        arrived(ctxbuf.at[s], r_ctx.at[s])
    for s in range(16):
        arrived(wb.at[s], r_b2.at[s])
    for d in range(1, 8):
        yy = (y + d) % 8
        arrived(wa.at[:, yy // 4, :, yy % 4], r_a2.at[yy])

    def project(core, half):
        buf = wa if half == 0 else wb
        total = None
        for s in range(2):
            if half == 0:
                block = buf[2 * s : 2 * s + 2].reshape(COLS, HALF)
            else:
                block = buf[8 * s : 8 * s + 8].reshape(COLS, HALF)
            term = mul(ctxbuf[2 * s + core], block, NN)
            total = term if total is None else total + term
        return total

    psend[:, 0:HALF] = project(o, 0)
    psend[:, HALF:] = project(o, 1)
    send(psend, precv, s_p.at[0], r_p.at[0], mate)
    stream_s[:, 0:HALF] = resid[:, 0:HALF].astype(f32) + project(c, 0)
    stream_s[:, HALF:] = resid[:, HALF:].astype(f32) + project(c, 1)
    arrived(precv, r_p.at[0])
    stream = stream_s[...] + precv[...]
    stream_s[...] = stream

    gains = gain[...]
    raw = None
    for part in parts_of(stream * gains, 3):
        term = mul(heads_t[...], part, NT)
        raw = term if raw is None else raw + term
    square = None
    for part in parts_of(stream * stream, 3):
        term = mul(jnp.ones((16, COLS), bf16), part, NT)
        square = term if square is None else square + term
    raw_rows = lax.broadcasted_iota(i32, (RAW, ROWS), 0)
    rawbuf[x] = jnp.where(
        raw_rows == A + 1, jnp.broadcast_to(square[0:1], (RAW, ROWS)), raw[0:RAW]
    )
    for d in (2, 1, 3):
        send(rawbuf.at[x], rawbuf.at[x], s_raw.at[d], r_raw.at[x], dev(d, 0, 0, c))
    for d in (1, 3, 2):
        xx = (x + d) % 4
        arrived(rawbuf.at[xx], r_raw.at[xx])
    raw = ((rawbuf[0] + rawbuf[1]) + rawbuf[2]) + rawbuf[3]

    inverse = lax.rsqrt(jnp.broadcast_to(raw[A + 1 : A + 2], (8, ROWS)) / D + epsilon)
    out = raw * jnp.broadcast_to(inverse[0:1], (RAW, ROWS))
    values = jnp.broadcast_to(out[A : A + 1], (8, ROWS))

    def later(v, n):
        return pltpu.roll(v, ROWS - n, 1)

    last = step == STEPS - 1
    next_values = jnp.where(last, 0.0, later(values, 1))
    delta = reward + discount * keep * next_values - values
    adv = valid * delta
    factor = jnp.where(last, 0.0, valid * (discount * trace_decay) * keep)
    adv = adv + factor * later(adv, 1)
    factor = factor * later(factor, 1)
    adv = adv + factor * later(adv, 2)
    factor = factor * later(factor, 2)
    adv = adv + factor * later(adv, 4)

    adv32 = jnp.broadcast_to(adv[0:1], (32, ROWS))
    valid32 = jnp.broadcast_to(valid[0:1], (32, ROWS))
    sums = jnp.sum(jnp.where(learner_hit, adv32, 0.0), axis=1, keepdims=True)
    counts = jnp.sum(jnp.where(learner_hit, valid32, 0.0), axis=1, keepdims=True)
    lane128 = lax.broadcasted_iota(i32, (32, 128), 1)
    sub128 = lax.broadcasted_iota(i32, (32, 128), 0)
    at_sum = lane128 == sub128
    at_count = lane128 == sub128 + 32
    message = jnp.sum(
        jnp.where(at_sum, sums, 0.0) + jnp.where(at_count, counts, 0.0), axis=0, keepdims=True
    )
    l1[me16] = message
    lsrc[...] = message
    for d in (4, 3, 5, 2, 6, 1, 7):
        for core in range(2):
            send(lsrc, l1.at[me16], s_l1.at[2 * d + core], r_l1.at[me16], dev(0, 0, d, core))
    send(lsrc, l1.at[me16], s_l1.at[0], r_l1.at[me16], mate)

    act_rows = raw_rows < A
    logits = jnp.where(act_rows, out, -1e30)
    top = jnp.max(logits, axis=0, keepdims=True)
    expo = jnp.where(act_rows, jnp.exp(logits - top), 0.0)
    prob = expo / jnp.sum(expo, axis=0, keepdims=True)
    chosen = raw_rows.astype(f32) == jnp.broadcast_to(action[0:1], (RAW, ROWS))
    score = prob - jnp.where(chosen, 1.0, 0.0)

    for s in range(1, 16):
        ss = (me16 + s) % 16
        arrived(l1.at[ss], r_l1.at[ss])
    total = l1[0]
    for s in range(1, 16):
        total = total + l1[s]
    l2[y] = total
    for d in (4, 3, 5, 2, 6, 1, 7):
        send(l2.at[y], l2.at[y], s_l2.at[d], r_l2.at[y], dev(0, d, 0, c))
    e8 = jnp.where(env, adv32, 0.0)
    adv_grid = None
    for part in parts_of(e8, 3):
        term = mul(part, spread, NT)
        adv_grid = term if adv_grid is None else adv_grid + term
    adv_out[...] = adv_grid
    for d in range(1, 8):
        yy = (y + d) % 8
        arrived(l2.at[yy], r_l2.at[yy])
    total = l2[0]
    for s in range(1, 8):
        total = total + l2[s]
    wide = jnp.broadcast_to(total, (32, 128))
    sums = jnp.sum(jnp.where(at_sum, wide, 0.0), axis=1, keepdims=True)
    counts = jnp.sum(jnp.where(at_count, wide, 0.0), axis=1, keepdims=True)
    means = sums / counts
    own = jnp.sum(jnp.where(sub128 == dp, means, 0.0), axis=0, keepdims=True)
    misc_out[...] = jnp.broadcast_to(own, (8, 128))

    mean_row = jnp.sum(jnp.where(learner_hit, means, 0.0), axis=0, keepdims=True)
    count_row = jnp.sum(jnp.where(learner_hit, counts, 0.0), axis=0, keepdims=True)
    weight = valid[0:1] / count_row
    centered = adv[0:1] - mean_row
    grad_value_row = -value_weight * weight * adv[0:1]
    grad_out = jnp.where(
        act_rows,
        (weight * centered) * score,
        jnp.where(raw_rows == A, jnp.broadcast_to(grad_value_row, (RAW, ROWS)), 0.0),
    )
    inner = jnp.sum(grad_out * raw, axis=0, keepdims=True)
    inv = inverse[0:1]
    coef = inv * inv * inv * inner / D
    scaled_out = grad_out * inv
    tall = jnp.concatenate(
        [scaled_out, jnp.broadcast_to(coef, (HP - RAW, ROWS))], axis=0
    )
    tall_rows = lax.broadcasted_iota(i32, (HP, ROWS), 0)
    tall = jnp.where(tall_rows <= RAW, tall, 0.0)
    tall_parts = parts_of(tall, 2)

    one_row = (lax.broadcasted_iota(i32, (HP, 128), 0) == RAW).astype(f32).astype(bf16)
    grad_normed = mul(tall_parts[0], heads_t[...], TN) + mul(tall_parts[1], heads_t[...], TN)
    coef_col = mul(tall_parts[0], one_row, TN) + mul(tall_parts[1], one_row, TN)
    stream = stream_s[...]
    coef_wide = jnp.concatenate([coef_col] * 4, axis=1)
    gstream[c] = (gains * grad_normed - stream * coef_wide).astype(bf16)
    send(gstream.at[c], gstream.at[c], s_g.at[0], r_g.at[0], mate)

    high, low = parts_of(stream, 2)
    q = mul(tall_parts[0], high, NN) + mul(tall_parts[0], low, NN) + mul(tall_parts[1], high, NN)
    for p in range(16):
        qsrc[p] = q[(p % 4) * 16 : (p % 4) * 16 + 16, (p // 4) * 128 : (p // 4) * 128 + 128]
    q1[me16] = qsrc[me16]
    for d in (4, 3, 5, 2, 6, 1, 7):
        for core in range(2):
            part = ((z + d) % 8) * 2 + core
            send(qsrc.at[part], q1.at[me16], s_q1.at[2 * d + core], r_q1.at[me16], dev(0, 0, d, core))
    send(qsrc.at[z * 2 + o], q1.at[me16], s_q1.at[0], r_q1.at[me16], mate)

    arrived(gstream.at[o], r_g.at[0])
    for s in range(2):
        block = mul(ctxbuf[2 * s], gstream[0], TN) + mul(ctxbuf[2 * s + 1], gstream[1], TN)
        pb[2 * s : 2 * s + 2] = block.astype(bf16).reshape(2, 2, 2, 4, 16, COLS)
    first_cols, last_cols = pl.ds(0, HALF), pl.ds(HALF, HALF)

    def send_z(src_of, dst, ssem, rsem):
        for s in range(4):
            away = (4 * c + s) != z
            dz = 4 * c + s - z + 8
            for core in range(2):
                copy = remote(src_of(s, core), dst, ssem.at[2 * s + core], rsem, dev(0, 0, dz, core))

                @pl.when(away)
                def _():
                    copy.start()

                pending.append((away, copy))
            own_copy = remote(src_of(s, o), dst, ssem.at[8], rsem, mate)

            @pl.when(jnp.logical_not(away))
            def _():
                pltpu.make_async_copy(src_of(s, c), dst, rsem).start()
                own_copy.start()

            pending.append((jnp.logical_not(away), own_copy))

    send_z(lambda s, core: pb.at[s, :, core, :, :, first_cols], ra.at[z], s_ra, r_ra.at[z])
    for d in (4, 3, 5, 2, 6, 1, 7):
        yy = (y + d) % 8
        send(
            pb.at[:, yy // 4, :, yy % 4, :, last_cols], rb.at[y], s_rb.at[d], r_rb.at[y], dev(0, d, 0, c)
        )
    rb[y] = pb[:, h, :, r, :, HALF:]

    for s in range(1, 16):
        ss = (me16 + s) % 16
        arrived(q1.at[ss], r_q1.at[ss])
    total = q1[0]
    for s in range(1, 16):
        total = total + q1[s]
    q2[y] = total
    for d in (4, 3, 5, 2, 6, 1, 7):
        send(q2.at[y], q2.at[y], s_q2.at[d], r_q2.at[y], dev(0, d, 0, c))
    for d in range(1, 8):
        yy = (y + d) % 8
        arrived(q2.at[yy], r_q2.at[yy])
    total = q2[0]
    for s in range(1, 8):
        total = total + q2[s]
    qf[me16] = total
    q2src[...] = total
    for d in (4, 3, 5, 2, 6, 1, 7):
        for core in range(2):
            send(q2src, qf.at[me16], s_q3.at[2 * d + core], r_q3.at[me16], dev(0, 0, d, core))
    send(q2src, qf.at[me16], s_q3.at[0], r_q3.at[me16], mate)

    for d in range(8):
        zz = (z + d) % 8
        arrived(ra.at[zz], r_ra.at[zz])
    total = ra[0].astype(f32)
    for s in range(1, 8):
        total = total + ra[s].astype(f32)
    sa2[...] = total
    for d in (4, 3, 5, 2, 6, 1, 7):
        yy = (y + d) % 8
        send(sa2.at[yy // 4, yy % 4], ra2.at[y], s_ra2.at[d], r_ra2.at[y], dev(0, d, 0, c))
    ra2[y] = sa2[h, r]
    for d in range(1, 8):
        yy = (y + d) % 8
        arrived(rb.at[yy], r_rb.at[yy])
    total = rb[0].astype(f32)
    for s in range(1, 8):
        total = total + rb[s].astype(f32)
    sb2[...] = total
    send_z(lambda s, core: sb2.at[s, core], rb2.at[z], s_rb2, r_rb2.at[z])
    for d in range(1, 8):
        yy = (y + d) % 8
        arrived(ra2.at[yy], r_ra2.at[yy])
    total = ra2[0]
    for s in range(1, 8):
        total = total + ra2[s]
    fin[r, :, 0:HALF] = total
    for d in range(8):
        zz = (z + d) % 8
        arrived(rb2.at[zz], r_rb2.at[zz])
    total = rb2[0]
    for s in range(1, 8):
        total = total + rb2[s]
    fin[r, :, HALF:] = total
    for d in (2, 1, 3):
        rr = (r + d) % 4
        device = {"role": rr, "dp": dp, "mp": x}
        send(fin.at[r], fin.at[r], s_f.at[d], r_f.at[r], device)

    for s in range(1, 16):
        ss = (me16 + s) % 16
        arrived(qf.at[ss], r_q3.at[ss])
    gain_rows = []
    for lane in range(4):
        cols = slice(lane * 128, lane * 128 + 128)
        block = jnp.concatenate([qf[lane * 4 + s] for s in range(3)], axis=0)
        gain_row = jnp.sum(block * heads_t[0:RAW, cols].astype(f32), axis=0, keepdims=True)
        rows = lax.broadcasted_iota(i32, (RAW, 128), 0)
        heads_out[:, cols] = jnp.where(
            rows == A + 1, jnp.broadcast_to(gain_row, (RAW, 128)), block * gains[:, cols]
        )

    for d in range(1, 4):
        rr = (r + d) % 4
        arrived(fin.at[rr], r_f.at[rr])
    for s in range(4):
        gw_out[16 * s : 16 * s + 16] = fin[s]

    for condition, copy in pending:
        if condition is None:
            copy.wait_send()
        else:
            pl.when(condition)(copy.wait_send)


def per_device(
    residual_in,
    context,
    w_out,
    norm_gain,
    policy_head,
    value_head,
    rewards,
    resets,
    actions,
    lengths,
    assignment,
):
    vmem = pl.BlockSpec(memory_space=pltpu.VMEM)
    dma = pltpu.SemaphoreType.DMA
    buffers = [
        pltpu.VMEM((4, ROWS, COLS), bf16),
        pltpu.VMEM((4, 2, 2, 4, 16, HALF), bf16),
        pltpu.VMEM((16, 64, HALF), bf16),
        pltpu.VMEM((64, HALF), bf16),
        pltpu.VMEM((ROWS, COLS), f32),
        pltpu.VMEM((ROWS, COLS), f32),
        pltpu.VMEM((ROWS, COLS), f32),
        pltpu.VMEM((2, ROWS, COLS), bf16),
        pltpu.VMEM((4, RAW, ROWS), f32),
        pltpu.VMEM((16, 1, 128), f32),
        pltpu.VMEM((8, 1, 128), f32),
        pltpu.VMEM((1, 128), f32),
        pltpu.VMEM((HP, COLS), bf16),
        pltpu.VMEM((16, 16, 128), f32),
        pltpu.VMEM((16, 16, 128), f32),
        pltpu.VMEM((8, 16, 128), f32),
        pltpu.VMEM((16, 128), f32),
        pltpu.VMEM((16, 16, 128), f32),
        pltpu.VMEM((4, 2, 2, 4, 16, COLS), bf16),
        pltpu.VMEM((8, 2, 4, 16, HALF), bf16),
        pltpu.VMEM((8, 4, 2, 16, HALF), bf16),
        pltpu.VMEM((2, 4, 16, HALF), f32),
        pltpu.VMEM((4, 2, 16, HALF), f32),
        pltpu.VMEM((8, 16, HALF), f32),
        pltpu.VMEM((8, 16, HALF), f32),
        pltpu.VMEM((4, 16, COLS), f32),
    ]
    counts = [4, 4, 8, 8, 8, 8, 1, 1, 16, 16, 1, 1, 4, 4, 16, 16, 8, 8, 1, 1]
    counts += [16, 16, 8, 8, 16, 16]
    counts += [9, 8, 8, 8, 8, 8, 9, 8, 4, 4]
    adv, misc, grad_w, heads = pl.pallas_call(
        kernel,
        out_shape=(
            jax.ShapeDtypeStruct((32, STEPS), f32),
            jax.ShapeDtypeStruct((8, 128), f32),
            jax.ShapeDtypeStruct((64, COLS), f32),
            jax.ShapeDtypeStruct((RAW, COLS), f32),
        ),
        in_specs=[vmem] * 11,
        out_specs=(vmem,) * 4,
        scratch_shapes=buffers + [dma((n,)) for n in counts],
        compiler_params=pltpu.CompilerParams(
            collective_id=0, has_side_effects=True, vmem_limit_bytes=48 * 1024 * 1024
        ),
        name="policy_step",
    )(
        residual_in.reshape(ROWS, COLS),
        context.reshape(ROWS, COLS),
        w_out,
        norm_gain.reshape(1, COLS),
        policy_head,
        value_head.reshape(1, COLS),
        rewards,
        resets,
        actions,
        lengths.reshape(1, 32),
        assignment.reshape(1, 32),
    )
    return (adv, misc[0, 0:1], grad_w, heads[A + 1], heads[0:A].T, heads[A])


def solution(mesh):
    placed = (
        P(("role", "dp"), None, "mp"),
        P(("role", "dp"), None, "mp"),
        P("dp", "mp"),
        P("mp"),
        P("mp", None),
        P("mp"),
        P(("role", "dp"), None),
        P(("role", "dp"), None),
        P(("role", "dp"), None),
        P(("role", "dp")),
        P(("role", "dp")),
    )
    return jax.shard_map(
        per_device,
        mesh=mesh,
        in_specs=placed,
        out_specs=(
            P(("role", "dp"), None),
            P("dp"),
            P("dp", "mp"),
            P("mp"),
            P("mp", None),
            P("mp"),
        ),
        check_vma=False,
    )
```

```python
import jax
import jax.numpy as jnp
from jax import lax
from jax.experimental import pallas as pl
from jax.experimental.pallas import tpu as pltpu
from jax.sharding import PartitionSpec as P

D = 2048
A = 43
STEPS = 8
ROWS = 256
COLS = 512
HALF = 256
HP = 64
RAW = 48

discount = 0.99
trace_decay = 0.95
value_weight = 0.5
epsilon = 1e-05

MESH = pl.DeviceIdType.MESH
bf16 = jnp.bfloat16
f32 = jnp.float32
i32 = jnp.int32

NN = (((1,), (0,)), ((), ()))
NT = (((1,), (1,)), ((), ()))
TN = (((0,), (0,)), ((), ()))


def mul(a, b, dims):
    return lax.dot_general(a, b, dims, preferred_element_type=f32)


def parts_of(a, n):
    out = []
    for _ in range(n):
        high = a.astype(bf16)
        out.append(high)
        a = a - high.astype(f32)
    return out


FAR_FIRST = (4, 3, 5, 2, 6, 1, 7)


def kernel(
    resid_h, ctx_h, w_h, gain_h, policy_h, value_h,
    rewards_h, resets_h, actions_h, lengths_h, assign_h,
    adv_out, misc_out, gw_out, heads_out,
    resid, gain, policy, value, rewards, resets, actions, lengths, assign,
    ctxbuf, ctx_t, wbuf, psend, precv, stream_s, gstream,
    rawbuf, l1, l2, lsrc, heads_t, qsrc, qmate, qsum, q1, q2, qf,
    pb, ra, rb, sa2, sb2, ra2, rb2,
    s_all, r_in, r_ctx, r_w, r_p, r_raw, r_l1, r_l2, r_g,
    r_q0, r_q1, r_q2, r_q3, r_q4, r_ra, r_rb, r_ra2, r_rb2, r_f,
):
    role = lax.axis_index("role")
    dp = lax.axis_index("dp")
    x = lax.axis_index("mp")
    z = dp // 4
    h = (dp // 2) % 2
    c = dp % 2
    y = h * 4 + role
    r = role
    o = 1 - c
    me16 = z * 2 + c

    def dev(dx, dy, dz, core):
        yy = (y + dy + 8) % 8
        return {
            "role": yy % 4,
            "dp": ((z + dz + 8) % 8) * 4 + (yy // 4) * 2 + core,
            "mp": (x + dx + 4) % 4,
        }

    mate = dev(0, 0, 0, o)
    pending = []

    def remote(src, dst, rsem, device):
        slot = len(pending)
        return pltpu.make_async_remote_copy(
            src_ref=src,
            dst_ref=dst,
            send_sem=s_all.at[slot],
            recv_sem=rsem,
            device_id=device,
            device_id_type=MESH,
        )

    def send(src, dst, rsem, device):
        copy = remote(src, dst, rsem, device)
        copy.start()
        pending.append((None, copy))

    def send_or_keep(here, src, dst, rsem, device):
        copy = remote(src, dst, rsem, device)
        away = jnp.logical_not(here)

        @pl.when(here)
        def _():
            pltpu.make_async_copy(src, dst, rsem).start()

        @pl.when(away)
        def _():
            copy.start()

        pending.append((away, copy))

    def arrived(dst, rsem):
        pltpu.make_async_copy(dst, dst, rsem).wait()

    small = [
        (gain_h, gain), (policy_h, policy), (value_h, value), (rewards_h, rewards),
        (resets_h, resets), (actions_h, actions), (lengths_h, lengths), (assign_h, assign),
        (resid_h, resid),
    ]
    for n, (src, dst) in enumerate(small):
        pltpu.make_async_copy(src, dst, r_in.at[n]).start()

    barrier = pltpu.get_barrier_semaphore()
    peers = [mate, dev(1, 0, 0, 0), dev(1, 0, 0, 1), dev(3, 0, 0, 0), dev(3, 0, 0, 1)]
    peers += [dev(0, 0, 1, c), dev(0, 0, 7, c)]
    peers += [dev(0, d, 0, c) for d in range(1, 8)]
    peers += [{"role": 3 - r, "dp": z * 4 + (1 - h) * 2 + o, "mp": x}]
    for peer in peers:
        pl.semaphore_signal(barrier, inc=1, device_id=peer, device_id_type=MESH)
    pl.semaphore_wait(barrier, len(peers))

    send_or_keep(c == h, w_h, wbuf.at[z, c], r_w.at[z * 2 + c], mate)
    mirror = {"role": 3 - r, "dp": z * 4 + (1 - h) * 2 + h, "mp": x}
    send(w_h, wbuf.at[z, c], r_w.at[z * 2 + c], mirror)

    def piece(zz, core):
        return ctx_h.at[:, pl.ds(pl.multiple_of(zz * 256 + core * 128, 128), 128)]

    def ctx_sem(m, cc, zz):
        return r_ctx.at[(m * 2 + cc) * 2 + zz]

    for first in range(2):
        for dx, zz in ((1, first), (3, 1 - first)):
            for core in range(2):
                send(piece(zz, core), ctxbuf.at[x, c, zz], ctx_sem(x, c, zz), dev(dx, 0, 0, core))
    for zz in range(2):
        pltpu.make_async_copy(piece(zz, c), ctxbuf.at[x, c, zz], ctx_sem(x, c, zz)).start()
        send(piece(zz, o), ctxbuf.at[x, c, zz], ctx_sem(x, c, zz), mate)

    up, down = dev(0, 0, 1, c), dev(0, 0, 7, c)

    def w_block(zz, cc):
        return wbuf.at[zz, cc], r_w.at[zz * 2 + cc]

    for cc in range(2):
        block, sem = w_block(z, cc)
        arrived(block, sem)
        send(block, block, sem, up)
        send(block, block, sem, down)

    for n in range(9):
        pltpu.make_async_copy(small[n][0], small[n][1], r_in.at[n]).wait()
    lane8 = lax.broadcasted_iota(i32, (8, ROWS), 1)
    sub8 = lax.broadcasted_iota(i32, (8, ROWS), 0)
    step = lane8 % STEPS
    own_step = step == sub8
    lane32 = lax.broadcasted_iota(i32, (32, ROWS), 1)
    sub32 = lax.broadcasted_iota(i32, (32, ROWS), 0)
    env_b = (lane32 // STEPS == sub32).astype(f32).astype(bf16)

    def to_row(grid):
        wide = jnp.where(own_step, mul(grid.astype(f32).astype(bf16), env_b, NN), 0.0)
        return jnp.broadcast_to(jnp.sum(wide, axis=0, keepdims=True), (8, ROWS))

    def env_row(vector):
        return mul(jnp.broadcast_to(vector.astype(f32), (8, 32)).astype(bf16), env_b, NN)

    reward = to_row(rewards[...])
    keep = 1.0 - to_row(resets[...])
    action = to_row(actions[...])
    length = env_row(lengths[...])
    learner = env_row(assign[...])
    valid = (step.astype(f32) < length).astype(f32)
    learner_hit = jnp.broadcast_to(learner[0:1], (32, ROWS)) == sub32.astype(f32)
    head_rows = lax.broadcasted_iota(i32, (HP, COLS), 0)
    heads_t[...] = jnp.where(
        head_rows == A,
        jnp.broadcast_to(value[...].astype(f32).reshape(1, COLS), (HP, COLS)),
        jnp.concatenate([policy[...].astype(f32), jnp.zeros((HP - A, COLS), f32)], axis=0),
    ).astype(bf16)

    for m, zz, dx in (((x + 3) % 4, 0, 1), ((x + 1) % 4, 1, 3)):
        for cc in range(2):
            block = ctxbuf.at[m, cc, zz]
            arrived(block, ctx_sem(m, cc, zz))
            send(block, block, ctx_sem(m, cc, zz), dev(dx, 0, 0, c))

    for s in range(1, 5):
        for cc in range(2):
            for sign, target, most in ((-1, up, 4 - cc), (1, down, 3 + cc)):
                if s <= most:
                    block, sem = w_block((z + sign * s + 8) % 8, cc)
                    arrived(block, sem)
                    if s < most:
                        send(block, block, sem, target)

    for cc in range(2):
        for zz in range(2):
            arrived(ctxbuf.at[x, cc, zz], ctx_sem(x, cc, zz))
            m = (x + 2) % 4
            arrived(ctxbuf.at[m, cc, zz], ctx_sem(m, cc, zz))
        m = (x + 3) % 4
        arrived(ctxbuf.at[m, cc, 1], ctx_sem(m, cc, 1))
        m = (x + 1) % 4
        arrived(ctxbuf.at[m, cc, 0], ctx_sem(m, cc, 0))

    def project(core):
        total = None
        for m in range(4):
            left = jnp.concatenate([ctxbuf[m, core, 0], ctxbuf[m, core, 1]], axis=1)
            term = mul(left, wbuf[2 * m : 2 * m + 2].reshape(256, COLS), NN)
            total = term if total is None else total + term
        return total

    psend[...] = project(o)
    send(psend, precv, r_p.at[0], mate)
    stream_s[...] = resid[...].astype(f32) + project(c)
    arrived(precv, r_p.at[0])
    stream = stream_s[...] + precv[...]
    stream_s[...] = stream

    gains = gain[...]
    raw = None
    for part in parts_of(stream * gains, 3):
        term = mul(heads_t[...], part, NT)
        raw = term if raw is None else raw + term
    square = None
    for part in parts_of(stream * stream, 3):
        term = mul(jnp.ones((16, COLS), bf16), part, NT)
        square = term if square is None else square + term
    raw_rows = lax.broadcasted_iota(i32, (RAW, ROWS), 0)
    rawbuf[x] = jnp.where(
        raw_rows == A + 1, jnp.broadcast_to(square[0:1], (RAW, ROWS)), raw[0:RAW]
    )
    for d in (2, 1, 3):
        send(rawbuf.at[x], rawbuf.at[x], r_raw.at[x], dev(d, 0, 0, c))
    for m in range(4):
        for zz in range(2):
            for cc in range(2):
                ctx_t[2 * m + zz, :, cc * ROWS : cc * ROWS + ROWS] = ctxbuf[m, cc, zz].T
    for d in (1, 3, 2):
        xx = (x + d) % 4
        arrived(rawbuf.at[xx], r_raw.at[xx])
    raw = ((rawbuf[0] + rawbuf[1]) + rawbuf[2]) + rawbuf[3]

    inverse = lax.rsqrt(jnp.broadcast_to(raw[A + 1 : A + 2], (8, ROWS)) / D + epsilon)
    out = raw * jnp.broadcast_to(inverse[0:1], (RAW, ROWS))
    values = jnp.broadcast_to(out[A : A + 1], (8, ROWS))

    def later(v, n):
        return pltpu.roll(v, ROWS - n, 1)

    last = step == STEPS - 1
    next_values = jnp.where(last, 0.0, later(values, 1))
    delta = reward + discount * keep * next_values - values
    adv = valid * delta
    factor = jnp.where(last, 0.0, valid * (discount * trace_decay) * keep)
    adv = adv + factor * later(adv, 1)
    factor = factor * later(factor, 1)
    adv = adv + factor * later(adv, 2)
    factor = factor * later(factor, 2)
    adv = adv + factor * later(adv, 4)

    adv32 = jnp.broadcast_to(adv[0:1], (32, ROWS))
    valid32 = jnp.broadcast_to(valid[0:1], (32, ROWS))
    sums = jnp.sum(jnp.where(learner_hit, adv32, 0.0), axis=1, keepdims=True)
    counts = jnp.sum(jnp.where(learner_hit, valid32, 0.0), axis=1, keepdims=True)
    lane128 = lax.broadcasted_iota(i32, (32, 128), 1)
    sub128 = lax.broadcasted_iota(i32, (32, 128), 0)
    at_sum = lane128 == sub128
    at_count = lane128 == sub128 + 32
    message = jnp.sum(
        jnp.where(at_sum, sums, 0.0) + jnp.where(at_count, counts, 0.0), axis=0, keepdims=True
    )
    l1[me16] = message
    lsrc[...] = message
    for d in FAR_FIRST:
        for core in range(2):
            send(lsrc, l1.at[me16], r_l1.at[me16], dev(0, 0, d, core))
    send(lsrc, l1.at[me16], r_l1.at[me16], mate)

    act_rows = raw_rows < A
    logits = jnp.where(act_rows, out, -1e30)
    top = jnp.max(logits, axis=0, keepdims=True)
    expo = jnp.where(act_rows, jnp.exp(logits - top), 0.0)
    prob = expo / jnp.sum(expo, axis=0, keepdims=True)
    chosen = raw_rows.astype(f32) == jnp.broadcast_to(action[0:1], (RAW, ROWS))
    score = prob - jnp.where(chosen, 1.0, 0.0)
    adv_grid = None
    for part in parts_of(jnp.where(own_step, adv, 0.0), 3):
        term = mul(part, env_b, NT)
        adv_grid = term if adv_grid is None else adv_grid + term
    adv_out[...] = adv_grid

    for s in range(1, 16):
        ss = (me16 + s) % 16
        arrived(l1.at[ss], r_l1.at[ss])
    total = l1[0]
    for s in range(1, 16):
        total = total + l1[s]
    l2[y] = total
    for d in FAR_FIRST:
        send(l2.at[y], l2.at[y], r_l2.at[y], dev(0, d, 0, c))
    for d in range(1, 8):
        yy = (y + d) % 8
        arrived(l2.at[yy], r_l2.at[yy])
    total = l2[0]
    for s in range(1, 8):
        total = total + l2[s]
    wide = jnp.broadcast_to(total, (32, 128))
    sums = jnp.sum(jnp.where(at_sum, wide, 0.0), axis=1, keepdims=True)
    counts = jnp.sum(jnp.where(at_count, wide, 0.0), axis=1, keepdims=True)
    means = sums / counts
    own = jnp.sum(jnp.where(sub128 == dp, means, 0.0), axis=0, keepdims=True)
    misc_out[...] = jnp.broadcast_to(own, (8, 128))

    mean_row = jnp.sum(jnp.where(learner_hit, means, 0.0), axis=0, keepdims=True)
    count_row = jnp.sum(jnp.where(learner_hit, counts, 0.0), axis=0, keepdims=True)
    weight = valid[0:1] / count_row
    centered = adv[0:1] - mean_row
    grad_value_row = -value_weight * weight * adv[0:1]
    grad_out = jnp.where(
        act_rows,
        (weight * centered) * score,
        jnp.where(raw_rows == A, jnp.broadcast_to(grad_value_row, (RAW, ROWS)), 0.0),
    )
    inner = jnp.sum(grad_out * raw, axis=0, keepdims=True)
    inv = inverse[0:1]
    coef = inv * inv * inv * inner / D
    scaled_out = grad_out * inv
    tall = jnp.concatenate([scaled_out, jnp.broadcast_to(coef, (HP - RAW, ROWS))], axis=0)
    tall_rows = lax.broadcasted_iota(i32, (HP, ROWS), 0)
    tall = jnp.where(tall_rows <= RAW, tall, 0.0)
    tall_parts = parts_of(tall, 2)

    one_row = (lax.broadcasted_iota(i32, (HP, 128), 0) == RAW).astype(f32).astype(bf16)
    grad_normed = mul(tall_parts[0], heads_t[...], TN) + mul(tall_parts[1], heads_t[...], TN)
    coef_col = mul(tall_parts[0], one_row, TN) + mul(tall_parts[1], one_row, TN)
    stream = stream_s[...]
    coef_wide = jnp.concatenate([coef_col] * 4, axis=1)
    gstream[c] = (gains * grad_normed - stream * coef_wide).astype(bf16)
    send(gstream.at[c], gstream.at[c], r_g.at[0], mate)

    high, low = parts_of(stream, 2)
    q = mul(tall_parts[0], high, NN) + mul(tall_parts[0], low, NN) + mul(tall_parts[1], high, NN)
    for p in range(16):
        qsrc[p % 2, p // 2] = q[
            (p % 4) * 16 : (p % 4) * 16 + 16, (p // 4) * 128 : (p // 4) * 128 + 128
        ]
    send(qsrc.at[o], qmate, r_q0.at[0], mate)

    arrived(gstream.at[o], r_g.at[0])
    first_cols, last_cols = pl.ds(0, HALF), pl.ds(HALF, HALF)
    grads = gstream[...].reshape(2 * ROWS, COLS)
    for d in FAR_FIRST + (0,):
        zz = (z + d) % 8
        block = mul(ctx_t[zz], grads, NN).astype(bf16).reshape(2, 4, 16, COLS)
        pb[zz] = block
        if d:
            send(pb.at[zz, :, :, :, first_cols], ra.at[z], r_ra.at[z], dev(0, 0, d, c))
        else:
            ra[z] = block[:, :, :, 0:HALF]

    def to_half(rr, core):
        here = jnp.logical_and(jnp.logical_and(h == c, r == rr), c == core)
        return here, {"role": rr, "dp": z * 4 + c * 2 + core, "mp": x}

    for core in range(2):
        for rr in range(4):
            here, device = to_half(rr, core)
            send_or_keep(here, pb.at[:, core, rr, :, last_cols], rb.at[y], r_rb.at[y], device)

    arrived(qmate, r_q0.at[0])
    qsum[...] = qsrc[c] + qmate[...]
    q1[z] = qsum[z]
    for d in FAR_FIRST:
        zz = (z + d) % 8
        send(qsum.at[zz], q1.at[z], r_q1.at[z], dev(0, 0, d, c))
    for d in range(1, 8):
        zz = (z + d) % 8
        arrived(q1.at[zz], r_q1.at[zz])
    total = q1[0]
    for s in range(1, 8):
        total = total + q1[s]
    q2[y] = total
    for d in FAR_FIRST:
        send(q2.at[y], q2.at[y], r_q2.at[y], dev(0, d, 0, c))

    for d in range(1, 8):
        zz = (z + d) % 8
        arrived(ra.at[zz], r_ra.at[zz])
    total = ra[0].astype(f32)
    for s in range(1, 8):
        total = total + ra[s].astype(f32)
    sa2[...] = total
    for core in range(2):
        for rr in range(4):
            here, device = to_half(rr, core)
            send_or_keep(here, sa2.at[core, rr], ra2.at[y], r_ra2.at[y], device)
    for s in range(8):
        arrived(rb.at[s], r_rb.at[s])
    total = rb[0].astype(f32)
    for s in range(1, 8):
        total = total + rb[s].astype(f32)
    sb2[...] = total
    rb2[z] = sb2[z]
    for d in FAR_FIRST:
        send(sb2.at[(z + d) % 8], rb2.at[z], r_rb2.at[z], dev(0, 0, d, c))

    for d in range(1, 8):
        yy = (y + d) % 8
        arrived(q2.at[yy], r_q2.at[yy])
    total = q2[0]
    for s in range(1, 8):
        total = total + q2[s]
    qf[c, z] = total
    for d in FAR_FIRST:
        send(qf.at[c, z], qf.at[c, z], r_q3.at[z], dev(0, 0, d, c))

    for s in range(8):
        arrived(ra2.at[s], r_ra2.at[s])
    total = ra2[0]
    for s in range(1, 8):
        total = total + ra2[s]
    gw_out[r, :, 0:HALF] = total
    for d in range(1, 8):
        zz = (z + d) % 8
        arrived(rb2.at[zz], r_rb2.at[zz])
    total = rb2[0]
    for s in range(1, 8):
        total = total + rb2[s]
    gw_out[r, :, HALF:] = total
    for d in (2, 1, 3):
        device = {"role": (r + d) % 4, "dp": dp, "mp": x}
        send(gw_out.at[r], gw_out.at[r], r_f.at[r], device)

    for d in range(1, 8):
        zz = (z + d) % 8
        arrived(qf.at[c, zz], r_q3.at[zz])
    send(qf.at[c], qf.at[c], r_q4.at[0], mate)
    arrived(qf.at[o], r_q4.at[0])
    rows = lax.broadcasted_iota(i32, (RAW, 128), 0)
    for lane in range(4):
        cols = slice(lane * 128, lane * 128 + 128)
        block = jnp.concatenate([qf[s % 2, lane * 2 + s // 2] for s in range(3)], axis=0)
        gain_row = jnp.sum(block * heads_t[0:RAW, cols].astype(f32), axis=0, keepdims=True)
        heads_out[:, cols] = jnp.where(
            rows == A + 1, jnp.broadcast_to(gain_row, (RAW, 128)), block * gains[:, cols]
        )

    for d in range(1, 4):
        rr = (r + d) % 4
        arrived(gw_out.at[rr], r_f.at[rr])

    for condition, copy in pending:
        if condition is None:
            copy.wait_send()
        else:
            pl.when(condition)(copy.wait_send)


def finish(adv, misc, gw, heads, adv_o, mean_o, gw_o, gain_o, policy_o, value_o):
    adv_o[...] = adv[...]
    mean_o[...] = misc[0:1, 0:1]
    gw_o[...] = gw[...].reshape(64, COLS)
    gain_o[...] = heads[A + 1 : A + 2]
    policy_o[...] = heads[0:A]
    value_o[...] = heads[A : A + 1]


def per_device(
    residual_in,
    context,
    w_out,
    norm_gain,
    policy_head,
    value_head,
    rewards,
    resets,
    actions,
    lengths,
    assignment,
):
    vmem = pl.BlockSpec(memory_space=pltpu.VMEM)
    hbm = pl.BlockSpec(memory_space=pltpu.HBM)
    dma = pltpu.SemaphoreType.DMA
    buffers = [
        pltpu.VMEM((ROWS, COLS), bf16),
        pltpu.VMEM((1, COLS), f32),
        pltpu.VMEM((A, COLS), bf16),
        pltpu.VMEM((COLS,), bf16),
        pltpu.VMEM((STEPS, 32), bf16),
        pltpu.VMEM((STEPS, 32), i32),
        pltpu.VMEM((STEPS, 32), i32),
        pltpu.VMEM((1, 32), i32),
        pltpu.VMEM((1, 32), i32),
        pltpu.VMEM((4, 2, 2, ROWS, 128), bf16),
        pltpu.VMEM((8, 128, 2 * ROWS), bf16),
        pltpu.VMEM((8, 2, 64, COLS), bf16),
        pltpu.VMEM((ROWS, COLS), f32),
        pltpu.VMEM((ROWS, COLS), f32),
        pltpu.VMEM((ROWS, COLS), f32),
        pltpu.VMEM((2, ROWS, COLS), bf16),
        pltpu.VMEM((4, RAW, ROWS), f32),
        pltpu.VMEM((16, 1, 128), f32),
        pltpu.VMEM((8, 1, 128), f32),
        pltpu.VMEM((1, 128), f32),
        pltpu.VMEM((HP, COLS), bf16),
        pltpu.VMEM((2, 8, 16, 128), f32),
        pltpu.VMEM((8, 16, 128), f32),
        pltpu.VMEM((8, 16, 128), f32),
        pltpu.VMEM((8, 16, 128), f32),
        pltpu.VMEM((8, 16, 128), f32),
        pltpu.VMEM((2, 8, 16, 128), f32),
        pltpu.VMEM((8, 2, 4, 16, COLS), bf16),
        pltpu.VMEM((8, 2, 4, 16, HALF), bf16),
        pltpu.VMEM((8, 8, 16, HALF), bf16),
        pltpu.VMEM((2, 4, 16, HALF), f32),
        pltpu.VMEM((8, 16, HALF), f32),
        pltpu.VMEM((8, 16, HALF), f32),
        pltpu.VMEM((8, 16, HALF), f32),
    ]
    counts = [160, 9, 16, 16, 1, 4, 16, 8, 1, 1, 8, 8, 8, 1, 8, 8, 8, 8, 4]
    step_out = pl.pallas_call(
        kernel,
        out_shape=(
            jax.ShapeDtypeStruct((STEPS, 32), f32),
            jax.ShapeDtypeStruct((8, 128), f32),
            jax.ShapeDtypeStruct((4, 16, COLS), f32),
            jax.ShapeDtypeStruct((RAW, COLS), f32),
        ),
        in_specs=[hbm] * 11,
        out_specs=(vmem,) * 4,
        scratch_shapes=buffers + [dma((n,)) for n in counts],
        compiler_params=pltpu.CompilerParams(
            collective_id=0, has_side_effects=True, vmem_limit_bytes=62 * 1024 * 1024
        ),
        name="policy_step",
    )(
        residual_in.reshape(ROWS, COLS),
        context.reshape(ROWS, COLS),
        w_out,
        norm_gain.reshape(1, COLS),
        policy_head.T,
        value_head,
        rewards.T,
        resets.T,
        actions.T,
        lengths.reshape(1, 32),
        assignment.reshape(1, 32),
    )
    adv, mean, grad_w, grad_gain, grad_policy, grad_value = pl.pallas_call(
        finish,
        out_shape=(
            jax.ShapeDtypeStruct((STEPS, 32), f32),
            jax.ShapeDtypeStruct((1, 1), f32),
            jax.ShapeDtypeStruct((64, COLS), f32),
            jax.ShapeDtypeStruct((1, COLS), f32),
            jax.ShapeDtypeStruct((A, COLS), f32),
            jax.ShapeDtypeStruct((1, COLS), f32),
        ),
        in_specs=[vmem] * 4,
        out_specs=(vmem,) * 6,
        name="write_outputs",
    )(*step_out)
    return (
        adv.T,
        mean.reshape(1),
        grad_w,
        grad_gain.reshape(COLS),
        grad_policy.T,
        grad_value.reshape(COLS),
    )


def solution(mesh):
    placed = (
        P(("role", "dp"), None, "mp"),
        P(("role", "dp"), None, "mp"),
        P("dp", "mp"),
        P("mp"),
        P("mp", None),
        P("mp"),
        P(("role", "dp"), None),
        P(("role", "dp"), None),
        P(("role", "dp"), None),
        P(("role", "dp")),
        P(("role", "dp")),
    )
    return jax.shard_map(
        per_device,
        mesh=mesh,
        in_specs=placed,
        out_specs=(
            P(("role", "dp"), None),
            P("dp"),
            P("dp", "mp"),
            P("mp"),
            P("mp", None),
            P("mp"),
        ),
        check_vma=False,
    )
```

```python
import jax
import jax.numpy as jnp
from jax import lax
from jax.experimental import pallas as pl
from jax.experimental.pallas import tpu as pltpu
from jax.sharding import PartitionSpec as P

D = 2048
A = 43
STEPS = 8
ROWS = 256
COLS = 512
HALF = 256
HP = 64
RAW = 48

discount = 0.99
trace_decay = 0.95
value_weight = 0.5
epsilon = 1e-05

MESH = pl.DeviceIdType.MESH
bf16 = jnp.bfloat16
f32 = jnp.float32
i32 = jnp.int32

NN = (((1,), (0,)), ((), ()))
NT = (((1,), (1,)), ((), ()))
TN = (((0,), (0,)), ((), ()))


def mul(a, b, dims):
    return lax.dot_general(a, b, dims, preferred_element_type=f32)


def parts_of(a, n):
    out = []
    for _ in range(n):
        high = a.astype(bf16)
        out.append(high)
        a = a - high.astype(f32)
    return out


FAR_FIRST = (4, 3, 5, 2, 6, 1, 7)


def kernel(
    resid_h, ctx_h, w_h, gain_h, policy_h, value_h,
    rewards_h, resets_h, actions_h, lengths_h, assign_h,
    adv_out, misc_out, gw_out, heads_out,
    resid, gain, policy, value, rewards, resets, actions, lengths, assign,
    ctxbuf, ctx_t, wbuf, psend, precv, stream_s, gstream,
    rawbuf, l1, l2, lsrc, heads_t, qsrc, qmate, qsum, q1, q2, qf,
    pb, ra, rb, sa2, sb2, ra2, rb2,
    s_all, r_in, r_ctx, r_w, r_wy, r_p, r_raw, r_l1, r_l2, r_g,
    r_q0, r_q1, r_q2, r_q3, r_q4, r_ra, r_rb, r_ra2, r_rb2, r_f,
):
    role = lax.axis_index("role")
    dp = lax.axis_index("dp")
    x = lax.axis_index("mp")
    z = dp // 4
    h = (dp // 2) % 2
    c = dp % 2
    y = h * 4 + role
    r = role
    o = 1 - c
    me16 = z * 2 + c

    def dev(dx, dy, dz, core):
        yy = (y + dy + 8) % 8
        return {
            "role": yy % 4,
            "dp": ((z + dz + 8) % 8) * 4 + (yy // 4) * 2 + core,
            "mp": (x + dx + 4) % 4,
        }

    mate = dev(0, 0, 0, o)
    pending = []

    def remote(src, dst, rsem, device):
        slot = len(pending)
        return pltpu.make_async_remote_copy(
            src_ref=src,
            dst_ref=dst,
            send_sem=s_all.at[slot],
            recv_sem=rsem,
            device_id=device,
            device_id_type=MESH,
        )

    def send(src, dst, rsem, device):
        copy = remote(src, dst, rsem, device)
        copy.start()
        pending.append((None, copy))

    def send_or_keep(here, src, dst, rsem, device):
        copy = remote(src, dst, rsem, device)
        away = jnp.logical_not(here)

        @pl.when(here)
        def _():
            pltpu.make_async_copy(src, dst, rsem).start()

        @pl.when(away)
        def _():
            copy.start()

        pending.append((away, copy))

    def arrived(dst, rsem):
        pltpu.make_async_copy(dst, dst, rsem).wait()

    small = [
        (gain_h, gain), (policy_h, policy), (value_h, value), (rewards_h, rewards),
        (resets_h, resets), (actions_h, actions), (lengths_h, lengths), (assign_h, assign),
        (resid_h, resid),
    ]
    for n, (src, dst) in enumerate(small):
        pltpu.make_async_copy(src, dst, r_in.at[n]).start()

    barrier = pltpu.get_barrier_semaphore()
    peers = [mate, dev(1, 0, 0, 0), dev(1, 0, 0, 1), dev(3, 0, 0, 0), dev(3, 0, 0, 1)]
    peers += [dev(0, 0, d, c) for d in (1, 2, 6, 7)]
    peers += [dev(0, d, 0, c) for d in range(1, 8)]
    peers += [{"role": 3 - r, "dp": z * 4 + (1 - h) * 2 + o, "mp": x}]
    for peer in peers:
        pl.semaphore_signal(barrier, inc=1, device_id=peer, device_id_type=MESH)
    pl.semaphore_wait(barrier, len(peers))

    mine = pl.ds(pl.multiple_of((y % 2) * HALF, HALF), HALF)
    theirs = pl.ds(pl.multiple_of((1 - y % 2) * HALF, HALF), HALF)
    mirror = {"role": 3 - r, "dp": z * 4 + (1 - h) * 2 + h, "mp": x}
    send(w_h.at[:, :, theirs], wbuf.at[z, c, :, :, theirs], r_w.at[z * 2 + c], mirror)
    send_or_keep(
        c == h, w_h.at[:, :, mine], wbuf.at[z, c, :, :, mine], r_w.at[z * 2 + c], mate
    )

    def piece(zz, core):
        return ctx_h.at[:, pl.ds(pl.multiple_of(zz * 256 + core * 128, 128), 128)]

    def ctx_sem(m, cc, zz):
        return r_ctx.at[(m * 2 + cc) * 2 + zz]

    for first in range(2):
        for dx, zz in ((1, first), (3, 1 - first)):
            for core in range(2):
                send(piece(zz, core), ctxbuf.at[x, c, zz], ctx_sem(x, c, zz), dev(dx, 0, 0, core))
    for zz in range(2):
        pltpu.make_async_copy(piece(zz, c), ctxbuf.at[x, c, zz], ctx_sem(x, c, zz)).start()
        send(piece(zz, o), ctxbuf.at[x, c, zz], ctx_sem(x, c, zz), mate)

    def w_block(zz, cc):
        return wbuf.at[zz, cc, :, :, mine], r_w.at[zz * 2 + cc]

    def to_y(zz, cc):
        block = wbuf.at[zz, cc, :, :, mine]
        send(block, block, r_wy.at[zz * 2 + cc], dev(0, 1 if cc == 0 else 7, 0, c))

    for cc in range(2):
        block, sem = w_block(z, cc)
        arrived(block, sem)
        for d in (2, 6, 1, 7):
            send(block, block, sem, dev(0, 0, d, c))
        to_y(z, cc)

    for n in range(9):
        pltpu.make_async_copy(small[n][0], small[n][1], r_in.at[n]).wait()
    lane8 = lax.broadcasted_iota(i32, (8, ROWS), 1)
    sub8 = lax.broadcasted_iota(i32, (8, ROWS), 0)
    step = lane8 % STEPS
    own_step = step == sub8
    lane32 = lax.broadcasted_iota(i32, (32, ROWS), 1)
    sub32 = lax.broadcasted_iota(i32, (32, ROWS), 0)
    env_b = (lane32 // STEPS == sub32).astype(f32).astype(bf16)

    def to_row(grid):
        wide = jnp.where(own_step, mul(grid.astype(f32).astype(bf16), env_b, NN), 0.0)
        return jnp.broadcast_to(jnp.sum(wide, axis=0, keepdims=True), (8, ROWS))

    def env_row(vector):
        return mul(jnp.broadcast_to(vector.astype(f32), (8, 32)).astype(bf16), env_b, NN)

    reward = to_row(rewards[...])
    keep = 1.0 - to_row(resets[...])
    action = to_row(actions[...])
    length = env_row(lengths[...])
    learner = env_row(assign[...])
    valid = (step.astype(f32) < length).astype(f32)
    learner_hit = jnp.broadcast_to(learner[0:1], (32, ROWS)) == sub32.astype(f32)
    head_rows = lax.broadcasted_iota(i32, (HP, COLS), 0)
    heads_t[...] = jnp.where(
        head_rows == A,
        jnp.broadcast_to(value[...].astype(f32).reshape(1, COLS), (HP, COLS)),
        jnp.concatenate([policy[...].astype(f32), jnp.zeros((HP - A, COLS), f32)], axis=0),
    ).astype(bf16)

    for m, zz, dx in (((x + 3) % 4, 0, 1), ((x + 1) % 4, 1, 3)):
        for cc in range(2):
            block = ctxbuf.at[m, cc, zz]
            arrived(block, ctx_sem(m, cc, zz))
            send(block, block, ctx_sem(m, cc, zz), dev(dx, 0, 0, c))

    for cc in range(2):
        for d in (6, 2):
            block, sem = w_block((z + d) % 8, cc)
            arrived(block, sem)
            if d == 6:
                if cc == 0:
                    send(block, block, sem, dev(0, 0, 2, c))
                send(block, block, sem, dev(0, 0, 1, c))
            else:
                if cc == 1:
                    send(block, block, sem, dev(0, 0, 6, c))
                send(block, block, sem, dev(0, 0, 7, c))
            to_y((z + d) % 8, cc)
    for d in (1, 7, 3, 5, 4):
        for cc in range(2):
            arrived(*w_block((z + d) % 8, cc))
            to_y((z + d) % 8, cc)

    for cc in range(2):
        for zz in range(2):
            arrived(ctxbuf.at[x, cc, zz], ctx_sem(x, cc, zz))
            m = (x + 2) % 4
            arrived(ctxbuf.at[m, cc, zz], ctx_sem(m, cc, zz))
        m = (x + 3) % 4
        arrived(ctxbuf.at[m, cc, 1], ctx_sem(m, cc, 1))
        m = (x + 1) % 4
        arrived(ctxbuf.at[m, cc, 0], ctx_sem(m, cc, 0))
    for s in range(8):
        for cc in range(2):
            arrived(wbuf.at[s, cc, :, :, theirs], r_wy.at[s * 2 + cc])

    def project(core):
        total = None
        for m in range(4):
            left = jnp.concatenate([ctxbuf[m, core, 0], ctxbuf[m, core, 1]], axis=1)
            term = mul(left, wbuf[2 * m : 2 * m + 2].reshape(256, COLS), NN)
            total = term if total is None else total + term
        return total

    psend[...] = project(o)
    send(psend, precv, r_p.at[0], mate)
    stream_s[...] = resid[...].astype(f32) + project(c)
    arrived(precv, r_p.at[0])
    stream = stream_s[...] + precv[...]
    stream_s[...] = stream

    gains = gain[...]
    raw = None
    for part in parts_of(stream * gains, 3):
        term = mul(heads_t[...], part, NT)
        raw = term if raw is None else raw + term
    square = None
    for part in parts_of(stream * stream, 3):
        term = mul(jnp.ones((16, COLS), bf16), part, NT)
        square = term if square is None else square + term
    raw_rows = lax.broadcasted_iota(i32, (RAW, ROWS), 0)
    rawbuf[x] = jnp.where(
        raw_rows == A + 1, jnp.broadcast_to(square[0:1], (RAW, ROWS)), raw[0:RAW]
    )
    for d in (2, 1, 3):
        send(rawbuf.at[x], rawbuf.at[x], r_raw.at[x], dev(d, 0, 0, c))
    for m in range(4):
        for zz in range(2):
            for cc in range(2):
                ctx_t[2 * m + zz, :, cc * ROWS : cc * ROWS + ROWS] = ctxbuf[m, cc, zz].T
    for d in (1, 3, 2):
        xx = (x + d) % 4
        arrived(rawbuf.at[xx], r_raw.at[xx])
    raw = ((rawbuf[0] + rawbuf[1]) + rawbuf[2]) + rawbuf[3]

    inverse = lax.rsqrt(jnp.broadcast_to(raw[A + 1 : A + 2], (8, ROWS)) / D + epsilon)
    out = raw * jnp.broadcast_to(inverse[0:1], (RAW, ROWS))
    values = jnp.broadcast_to(out[A : A + 1], (8, ROWS))

    def later(v, n):
        return pltpu.roll(v, ROWS - n, 1)

    last = step == STEPS - 1
    next_values = jnp.where(last, 0.0, later(values, 1))
    delta = reward + discount * keep * next_values - values
    adv = valid * delta
    factor = jnp.where(last, 0.0, valid * (discount * trace_decay) * keep)
    adv = adv + factor * later(adv, 1)
    factor = factor * later(factor, 1)
    adv = adv + factor * later(adv, 2)
    factor = factor * later(factor, 2)
    adv = adv + factor * later(adv, 4)

    adv32 = jnp.broadcast_to(adv[0:1], (32, ROWS))
    valid32 = jnp.broadcast_to(valid[0:1], (32, ROWS))
    sums = jnp.sum(jnp.where(learner_hit, adv32, 0.0), axis=1, keepdims=True)
    counts = jnp.sum(jnp.where(learner_hit, valid32, 0.0), axis=1, keepdims=True)
    lane128 = lax.broadcasted_iota(i32, (32, 128), 1)
    sub128 = lax.broadcasted_iota(i32, (32, 128), 0)
    at_sum = lane128 == sub128
    at_count = lane128 == sub128 + 32
    message = jnp.sum(
        jnp.where(at_sum, sums, 0.0) + jnp.where(at_count, counts, 0.0), axis=0, keepdims=True
    )
    l1[me16] = message
    lsrc[...] = message
    for d in FAR_FIRST:
        for core in range(2):
            send(lsrc, l1.at[me16], r_l1.at[me16], dev(0, 0, d, core))
    send(lsrc, l1.at[me16], r_l1.at[me16], mate)

    act_rows = raw_rows < A
    logits = jnp.where(act_rows, out, -1e30)
    top = jnp.max(logits, axis=0, keepdims=True)
    expo = jnp.where(act_rows, jnp.exp(logits - top), 0.0)
    prob = expo / jnp.sum(expo, axis=0, keepdims=True)
    chosen = raw_rows.astype(f32) == jnp.broadcast_to(action[0:1], (RAW, ROWS))
    score = prob - jnp.where(chosen, 1.0, 0.0)
    adv_grid = None
    for part in parts_of(jnp.where(own_step, adv, 0.0), 3):
        term = mul(part, env_b, NT)
        adv_grid = term if adv_grid is None else adv_grid + term
    adv_out[...] = adv_grid

    for s in range(1, 16):
        ss = (me16 + s) % 16
        arrived(l1.at[ss], r_l1.at[ss])
    total = l1[0]
    for s in range(1, 16):
        total = total + l1[s]
    l2[y] = total
    for d in FAR_FIRST:
        send(l2.at[y], l2.at[y], r_l2.at[y], dev(0, d, 0, c))
    for d in range(1, 8):
        yy = (y + d) % 8
        arrived(l2.at[yy], r_l2.at[yy])
    total = l2[0]
    for s in range(1, 8):
        total = total + l2[s]
    wide = jnp.broadcast_to(total, (32, 128))
    sums = jnp.sum(jnp.where(at_sum, wide, 0.0), axis=1, keepdims=True)
    counts = jnp.sum(jnp.where(at_count, wide, 0.0), axis=1, keepdims=True)
    means = sums / counts
    own = jnp.sum(jnp.where(sub128 == dp, means, 0.0), axis=0, keepdims=True)
    misc_out[...] = jnp.broadcast_to(own, (8, 128))

    mean_row = jnp.sum(jnp.where(learner_hit, means, 0.0), axis=0, keepdims=True)
    count_row = jnp.sum(jnp.where(learner_hit, counts, 0.0), axis=0, keepdims=True)
    weight = valid[0:1] / count_row
    centered = adv[0:1] - mean_row
    grad_value_row = -value_weight * weight * adv[0:1]
    grad_out = jnp.where(
        act_rows,
        (weight * centered) * score,
        jnp.where(raw_rows == A, jnp.broadcast_to(grad_value_row, (RAW, ROWS)), 0.0),
    )
    inner = jnp.sum(grad_out * raw, axis=0, keepdims=True)
    inv = inverse[0:1]
    coef = inv * inv * inv * inner / D
    scaled_out = grad_out * inv
    tall = jnp.concatenate([scaled_out, jnp.broadcast_to(coef, (HP - RAW, ROWS))], axis=0)
    tall_rows = lax.broadcasted_iota(i32, (HP, ROWS), 0)
    tall = jnp.where(tall_rows <= RAW, tall, 0.0)
    tall_parts = parts_of(tall, 2)

    one_row = (lax.broadcasted_iota(i32, (HP, 128), 0) == RAW).astype(f32).astype(bf16)
    grad_normed = mul(tall_parts[0], heads_t[...], TN) + mul(tall_parts[1], heads_t[...], TN)
    coef_col = mul(tall_parts[0], one_row, TN) + mul(tall_parts[1], one_row, TN)
    stream = stream_s[...]
    coef_wide = jnp.concatenate([coef_col] * 4, axis=1)
    gstream[c] = (gains * grad_normed - stream * coef_wide).astype(bf16)
    send(gstream.at[c], gstream.at[c], r_g.at[0], mate)

    high, low = parts_of(stream, 2)
    q = mul(tall_parts[0], high, NN) + mul(tall_parts[0], low, NN) + mul(tall_parts[1], high, NN)
    for p in range(16):
        qsrc[p % 2, p // 2] = q[
            (p % 4) * 16 : (p % 4) * 16 + 16, (p // 4) * 128 : (p // 4) * 128 + 128
        ]
    send(qsrc.at[o], qmate, r_q0.at[0], mate)

    arrived(qmate, r_q0.at[0])
    qsum[...] = qsrc[c] + qmate[...]
    q1[z] = qsum[z]
    for d in FAR_FIRST:
        zz = (z + d) % 8
        send(qsum.at[zz], q1.at[z], r_q1.at[z], dev(0, 0, d, c))

    arrived(gstream.at[o], r_g.at[0])
    first_cols, last_cols = pl.ds(0, HALF), pl.ds(HALF, HALF)
    grads = gstream[...].reshape(2 * ROWS, COLS)
    for d in FAR_FIRST + (0,):
        zz = (z + d) % 8
        block = mul(ctx_t[zz], grads, NN).astype(bf16).reshape(2, 4, 16, COLS)
        pb[zz] = block
        if d:
            send(pb.at[zz, :, :, :, first_cols], ra.at[z], r_ra.at[z], dev(0, 0, d, c))
        else:
            ra[z] = block[:, :, :, 0:HALF]

    def to_half(rr, core):
        here = jnp.logical_and(jnp.logical_and(h == c, r == rr), c == core)
        return here, {"role": rr, "dp": z * 4 + c * 2 + core, "mp": x}

    for core in range(2):
        for rr in range(4):
            here, device = to_half(rr, core)
            send_or_keep(here, pb.at[:, core, rr, :, last_cols], rb.at[y], r_rb.at[y], device)

    for d in range(1, 8):
        zz = (z + d) % 8
        arrived(q1.at[zz], r_q1.at[zz])
    total = q1[0]
    for s in range(1, 8):
        total = total + q1[s]
    q2[y] = total
    for d in FAR_FIRST:
        send(q2.at[y], q2.at[y], r_q2.at[y], dev(0, d, 0, c))

    for d in range(1, 8):
        zz = (z + d) % 8
        arrived(ra.at[zz], r_ra.at[zz])
    total = ra[0].astype(f32)
    for s in range(1, 8):
        total = total + ra[s].astype(f32)
    sa2[...] = total
    for core in range(2):
        for rr in range(4):
            here, device = to_half(rr, core)
            send_or_keep(here, sa2.at[core, rr], ra2.at[y], r_ra2.at[y], device)
    for s in range(8):
        arrived(rb.at[s], r_rb.at[s])
    total = rb[0].astype(f32)
    for s in range(1, 8):
        total = total + rb[s].astype(f32)
    sb2[...] = total
    rb2[z] = sb2[z]
    for d in FAR_FIRST:
        send(sb2.at[(z + d) % 8], rb2.at[z], r_rb2.at[z], dev(0, 0, d, c))

    for d in range(1, 8):
        yy = (y + d) % 8
        arrived(q2.at[yy], r_q2.at[yy])
    total = q2[0]
    for s in range(1, 8):
        total = total + q2[s]
    qf[c, z] = total
    for d in FAR_FIRST:
        send(qf.at[c, z], qf.at[c, z], r_q3.at[z], dev(0, 0, d, c))

    for s in range(8):
        arrived(ra2.at[s], r_ra2.at[s])
    total = ra2[0]
    for s in range(1, 8):
        total = total + ra2[s]
    gw_out[r, :, 0:HALF] = total
    for d in range(1, 8):
        zz = (z + d) % 8
        arrived(rb2.at[zz], r_rb2.at[zz])
    total = rb2[0]
    for s in range(1, 8):
        total = total + rb2[s]
    gw_out[r, :, HALF:] = total
    for d in (2, 1, 3):
        device = {"role": (r + d) % 4, "dp": dp, "mp": x}
        send(gw_out.at[r], gw_out.at[r], r_f.at[r], device)

    for d in range(1, 8):
        zz = (z + d) % 8
        arrived(qf.at[c, zz], r_q3.at[zz])
    send(qf.at[c], qf.at[c], r_q4.at[0], mate)
    arrived(qf.at[o], r_q4.at[0])
    rows = lax.broadcasted_iota(i32, (RAW, 128), 0)
    for lane in range(4):
        cols = slice(lane * 128, lane * 128 + 128)
        block = jnp.concatenate([qf[s % 2, lane * 2 + s // 2] for s in range(3)], axis=0)
        gain_row = jnp.sum(block * heads_t[0:RAW, cols].astype(f32), axis=0, keepdims=True)
        heads_out[:, cols] = jnp.where(
            rows == A + 1, jnp.broadcast_to(gain_row, (RAW, 128)), block * gains[:, cols]
        )

    for d in range(1, 4):
        rr = (r + d) % 4
        arrived(gw_out.at[rr], r_f.at[rr])

    for condition, copy in pending:
        if condition is None:
            copy.wait_send()
        else:
            pl.when(condition)(copy.wait_send)


def finish(adv, misc, gw, heads, adv_o, mean_o, gw_o, gain_o, policy_o, value_o):
    adv_o[...] = adv[...]
    mean_o[...] = misc[0:1, 0:1]
    gw_o[...] = gw[...].reshape(64, COLS)
    gain_o[...] = heads[A + 1 : A + 2]
    policy_o[...] = heads[0:A]
    value_o[...] = heads[A : A + 1]


def per_device(
    residual_in,
    context,
    w_out,
    norm_gain,
    policy_head,
    value_head,
    rewards,
    resets,
    actions,
    lengths,
    assignment,
):
    vmem = pl.BlockSpec(memory_space=pltpu.VMEM)
    hbm = pl.BlockSpec(memory_space=pltpu.HBM)
    dma = pltpu.SemaphoreType.DMA
    buffers = [
        pltpu.VMEM((ROWS, COLS), bf16),
        pltpu.VMEM((1, COLS), f32),
        pltpu.VMEM((A, COLS), bf16),
        pltpu.VMEM((COLS,), bf16),
        pltpu.VMEM((STEPS, 32), bf16),
        pltpu.VMEM((STEPS, 32), i32),
        pltpu.VMEM((STEPS, 32), i32),
        pltpu.VMEM((1, 32), i32),
        pltpu.VMEM((1, 32), i32),
        pltpu.VMEM((4, 2, 2, ROWS, 128), bf16),
        pltpu.VMEM((8, 128, 2 * ROWS), bf16),
        pltpu.VMEM((8, 2, 4, 16, COLS), bf16),
        pltpu.VMEM((ROWS, COLS), f32),
        pltpu.VMEM((ROWS, COLS), f32),
        pltpu.VMEM((ROWS, COLS), f32),
        pltpu.VMEM((2, ROWS, COLS), bf16),
        pltpu.VMEM((4, RAW, ROWS), f32),
        pltpu.VMEM((16, 1, 128), f32),
        pltpu.VMEM((8, 1, 128), f32),
        pltpu.VMEM((1, 128), f32),
        pltpu.VMEM((HP, COLS), bf16),
        pltpu.VMEM((2, 8, 16, 128), f32),
        pltpu.VMEM((8, 16, 128), f32),
        pltpu.VMEM((8, 16, 128), f32),
        pltpu.VMEM((8, 16, 128), f32),
        pltpu.VMEM((8, 16, 128), f32),
        pltpu.VMEM((2, 8, 16, 128), f32),
        pltpu.VMEM((8, 2, 4, 16, COLS), bf16),
        pltpu.VMEM((8, 2, 4, 16, HALF), bf16),
        pltpu.VMEM((8, 8, 16, HALF), bf16),
        pltpu.VMEM((2, 4, 16, HALF), f32),
        pltpu.VMEM((8, 16, HALF), f32),
        pltpu.VMEM((8, 16, HALF), f32),
        pltpu.VMEM((8, 16, HALF), f32),
    ]
    counts = [160, 9, 16, 16, 16, 1, 4, 16, 8, 1, 1, 8, 8, 8, 1, 8, 8, 8, 8, 4]
    step_out = pl.pallas_call(
        kernel,
        out_shape=(
            jax.ShapeDtypeStruct((STEPS, 32), f32),
            jax.ShapeDtypeStruct((8, 128), f32),
            jax.ShapeDtypeStruct((4, 16, COLS), f32),
            jax.ShapeDtypeStruct((RAW, COLS), f32),
        ),
        in_specs=[hbm] * 11,
        out_specs=(vmem,) * 4,
        scratch_shapes=buffers + [dma((n,)) for n in counts],
        compiler_params=pltpu.CompilerParams(
            collective_id=0, has_side_effects=True, vmem_limit_bytes=62 * 1024 * 1024
        ),
        name="policy_step",
    )(
        residual_in.reshape(ROWS, COLS),
        context.reshape(ROWS, COLS),
        w_out.reshape(4, 16, COLS),
        norm_gain.reshape(1, COLS),
        policy_head.T,
        value_head,
        rewards.T,
        resets.T,
        actions.T,
        lengths.reshape(1, 32),
        assignment.reshape(1, 32),
    )
    adv, mean, grad_w, grad_gain, grad_policy, grad_value = pl.pallas_call(
        finish,
        out_shape=(
            jax.ShapeDtypeStruct((STEPS, 32), f32),
            jax.ShapeDtypeStruct((1, 1), f32),
            jax.ShapeDtypeStruct((64, COLS), f32),
            jax.ShapeDtypeStruct((1, COLS), f32),
            jax.ShapeDtypeStruct((A, COLS), f32),
            jax.ShapeDtypeStruct((1, COLS), f32),
        ),
        in_specs=[vmem] * 4,
        out_specs=(vmem,) * 6,
        name="write_outputs",
    )(*step_out)
    return (
        adv.T,
        mean.reshape(1),
        grad_w,
        grad_gain.reshape(COLS),
        grad_policy.T,
        grad_value.reshape(COLS),
    )


def solution(mesh):
    placed = (
        P(("role", "dp"), None, "mp"),
        P(("role", "dp"), None, "mp"),
        P("dp", "mp"),
        P("mp"),
        P("mp", None),
        P("mp"),
        P(("role", "dp"), None),
        P(("role", "dp"), None),
        P(("role", "dp"), None),
        P(("role", "dp")),
        P(("role", "dp")),
    )
    return jax.shard_map(
        per_device,
        mesh=mesh,
        in_specs=placed,
        out_specs=(
            P(("role", "dp"), None),
            P("dp"),
            P("dp", "mp"),
            P("mp"),
            P("mp", None),
            P("mp"),
        ),
        check_vma=False,
    )
```

```python
import jax
import jax.numpy as jnp
from jax import lax
from jax.experimental import pallas as pl
from jax.experimental.pallas import tpu as pltpu
from jax.sharding import PartitionSpec as P

D = 2048
A = 43
STEPS = 8
ROWS = 256
COLS = 512
HALF = 256
HP = 64
RAW = 48

discount = 0.99
trace_decay = 0.95
value_weight = 0.5
epsilon = 1e-05

MESH = pl.DeviceIdType.MESH
bf16 = jnp.bfloat16
f32 = jnp.float32
i32 = jnp.int32

NN = (((1,), (0,)), ((), ()))
NT = (((1,), (1,)), ((), ()))
TN = (((0,), (0,)), ((), ()))


def mul(a, b, dims):
    return lax.dot_general(a, b, dims, preferred_element_type=f32)


def parts_of(a, n):
    out = []
    for _ in range(n):
        high = a.astype(bf16)
        out.append(high)
        a = a - high.astype(f32)
    return out


FAR_FIRST = (4, 3, 5, 2, 6, 1, 7)


def kernel(
    resid_h, ctx_h, w_h, gain_h, policy_h, value_h,
    rewards_h, resets_h, actions_h, lengths_h, assign_h,
    adv_out, misc_out, gw_out, heads_out,
    resid, gain, policy, value, rewards, resets, actions, lengths, assign,
    ctxbuf, ctx_t, wbuf, psend, precv, stream_s, gstream,
    rawbuf, l1, l2, lsrc, heads_t, qsrc, qmate, qsum, q1, q2, qf,
    pb, ra, rb, sa2, sb2, ra2, rb2,
    s_all, r_in, r_ctx, r_w, r_wy, r_p, r_raw, r_l1, r_l2, r_g,
    r_q0, r_q1, r_q2, r_q3, r_q4, r_ra, r_rb, r_ra2, r_rb2, r_f, tokens,
):
    role = lax.axis_index("role")
    dp = lax.axis_index("dp")
    x = lax.axis_index("mp")
    z = dp // 4
    h = (dp // 2) % 2
    c = dp % 2
    y = h * 4 + role
    r = role
    o = 1 - c
    me16 = z * 2 + c

    def dev(dx, dy, dz, core):
        yy = (y + dy + 8) % 8
        return {
            "role": yy % 4,
            "dp": ((z + dz + 8) % 8) * 4 + (yy // 4) * 2 + core,
            "mp": (x + dx + 4) % 4,
        }

    mate = dev(0, 0, 0, o)
    pending = []

    def remote(src, dst, rsem, device):
        slot = len(pending)
        return pltpu.make_async_remote_copy(
            src_ref=src,
            dst_ref=dst,
            send_sem=s_all.at[slot],
            recv_sem=rsem,
            device_id=device,
            device_id_type=MESH,
        )

    def send(src, dst, rsem, device):
        copy = remote(src, dst, rsem, device)
        copy.start()
        pending.append((None, copy))

    def send_or_keep(here, src, dst, rsem, device):
        copy = remote(src, dst, rsem, device)
        away = jnp.logical_not(here)

        @pl.when(here)
        def _():
            pltpu.make_async_copy(src, dst, rsem).start()

        @pl.when(away)
        def _():
            copy.start()

        pending.append((away, copy))

    def arrived(dst, rsem):
        pltpu.make_async_copy(dst, dst, rsem).wait()

    small = [
        (gain_h, gain), (policy_h, policy), (value_h, value), (rewards_h, rewards),
        (resets_h, resets), (actions_h, actions), (lengths_h, lengths), (assign_h, assign),
        (resid_h, resid),
    ]
    for n, (src, dst) in enumerate(small):
        pltpu.make_async_copy(src, dst, r_in.at[n]).start()

    barrier = pltpu.get_barrier_semaphore()
    peers = [mate, dev(1, 0, 0, 0), dev(1, 0, 0, 1), dev(3, 0, 0, 0), dev(3, 0, 0, 1)]
    peers += [dev(0, 0, d, c) for d in (1, 2, 6, 7)]
    peers += [dev(0, 1, 0, c), dev(0, 7, 0, c)]
    peers += [{"role": 3 - r, "dp": z * 4 + (1 - h) * 2 + core, "mp": x} for core in range(2)]
    for peer in peers:
        pl.semaphore_signal(barrier, inc=1, device_id=peer, device_id_type=MESH)
    pl.semaphore_wait(barrier, len(peers))

    def tell(n):
        pl.semaphore_signal(tokens.at[2 * n], inc=1, device_id=dev(0, 1, 0, c), device_id_type=MESH)
        pl.semaphore_signal(
            tokens.at[2 * n + 1], inc=1, device_id=dev(0, 7, 0, c), device_id_type=MESH
        )

    def hear(n):
        pl.semaphore_wait(tokens.at[2 * n], 1)
        pl.semaphore_wait(tokens.at[2 * n + 1], 1)

    tell(0)

    mine = pl.ds(pl.multiple_of((y % 2) * HALF, HALF), HALF)
    theirs = pl.ds(pl.multiple_of((1 - y % 2) * HALF, HALF), HALF)
    mirror = {"role": 3 - r, "dp": z * 4 + (1 - h) * 2 + h, "mp": x}
    send(w_h.at[:, :, theirs], wbuf.at[z, c, :, :, theirs], r_w.at[z * 2 + c], mirror)
    send_or_keep(
        c == h, w_h.at[:, :, mine], wbuf.at[z, c, :, :, mine], r_w.at[z * 2 + c], mate
    )

    def piece(zz, core):
        return ctx_h.at[:, pl.ds(pl.multiple_of(zz * 256 + core * 128, 128), 128)]

    def ctx_sem(m, cc, zz):
        return r_ctx.at[(m * 2 + cc) * 2 + zz]

    for first in range(2):
        for dx, zz in ((1, first), (3, 1 - first)):
            for core in range(2):
                send(piece(zz, core), ctxbuf.at[x, c, zz], ctx_sem(x, c, zz), dev(dx, 0, 0, core))
    for zz in range(2):
        pltpu.make_async_copy(piece(zz, c), ctxbuf.at[x, c, zz], ctx_sem(x, c, zz)).start()
        send(piece(zz, o), ctxbuf.at[x, c, zz], ctx_sem(x, c, zz), mate)

    def w_block(zz, cc):
        return wbuf.at[zz, cc, :, :, mine], r_w.at[zz * 2 + cc]

    def to_y(zz, cc):
        block = wbuf.at[zz, cc, :, :, mine]
        send(block, block, r_wy.at[zz * 2 + cc], dev(0, 1 if cc == 0 else 7, 0, c))

    for cc in range(2):
        block, sem = w_block(z, cc)
        arrived(block, sem)
        for d in (2, 6, 1, 7):
            send(block, block, sem, dev(0, 0, d, c))
        to_y(z, cc)

    for n in range(9):
        pltpu.make_async_copy(small[n][0], small[n][1], r_in.at[n]).wait()
    lane8 = lax.broadcasted_iota(i32, (8, ROWS), 1)
    sub8 = lax.broadcasted_iota(i32, (8, ROWS), 0)
    step = lane8 % STEPS
    own_step = step == sub8
    lane32 = lax.broadcasted_iota(i32, (32, ROWS), 1)
    sub32 = lax.broadcasted_iota(i32, (32, ROWS), 0)
    env_b = (lane32 // STEPS == sub32).astype(f32).astype(bf16)

    def to_row(grid):
        wide = jnp.where(own_step, mul(grid.astype(f32).astype(bf16), env_b, NN), 0.0)
        return jnp.broadcast_to(jnp.sum(wide, axis=0, keepdims=True), (8, ROWS))

    def env_row(vector):
        return mul(jnp.broadcast_to(vector.astype(f32), (8, 32)).astype(bf16), env_b, NN)

    reward = to_row(rewards[...])
    keep = 1.0 - to_row(resets[...])
    action = to_row(actions[...])
    length = env_row(lengths[...])
    learner = env_row(assign[...])
    valid = (step.astype(f32) < length).astype(f32)
    learner_hit = jnp.broadcast_to(learner[0:1], (32, ROWS)) == sub32.astype(f32)
    head_rows = lax.broadcasted_iota(i32, (HP, COLS), 0)
    heads_t[...] = jnp.where(
        head_rows == A,
        jnp.broadcast_to(value[...].astype(f32).reshape(1, COLS), (HP, COLS)),
        jnp.concatenate([policy[...].astype(f32), jnp.zeros((HP - A, COLS), f32)], axis=0),
    ).astype(bf16)

    for m, zz, dx in (((x + 3) % 4, 0, 1), ((x + 1) % 4, 1, 3)):
        for cc in range(2):
            block = ctxbuf.at[m, cc, zz]
            arrived(block, ctx_sem(m, cc, zz))
            send(block, block, ctx_sem(m, cc, zz), dev(dx, 0, 0, c))

    hear(0)
    tell(1)
    for cc in range(2):
        for d in (6, 2):
            block, sem = w_block((z + d) % 8, cc)
            arrived(block, sem)
            if d == 6:
                if cc == 0:
                    send(block, block, sem, dev(0, 0, 2, c))
                send(block, block, sem, dev(0, 0, 1, c))
            else:
                if cc == 1:
                    send(block, block, sem, dev(0, 0, 6, c))
                send(block, block, sem, dev(0, 0, 7, c))
            to_y((z + d) % 8, cc)
    hear(1)
    tell(2)
    for d in (1, 7, 3, 5, 4):
        for cc in range(2):
            arrived(*w_block((z + d) % 8, cc))
            to_y((z + d) % 8, cc)

    for cc in range(2):
        for zz in range(2):
            arrived(ctxbuf.at[x, cc, zz], ctx_sem(x, cc, zz))
            m = (x + 2) % 4
            arrived(ctxbuf.at[m, cc, zz], ctx_sem(m, cc, zz))
        m = (x + 3) % 4
        arrived(ctxbuf.at[m, cc, 1], ctx_sem(m, cc, 1))
        m = (x + 1) % 4
        arrived(ctxbuf.at[m, cc, 0], ctx_sem(m, cc, 0))
    hear(2)
    for s in range(8):
        for cc in range(2):
            arrived(wbuf.at[s, cc, :, :, theirs], r_wy.at[s * 2 + cc])

    def project(core):
        total = None
        for m in range(4):
            left = jnp.concatenate([ctxbuf[m, core, 0], ctxbuf[m, core, 1]], axis=1)
            term = mul(left, wbuf[2 * m : 2 * m + 2].reshape(256, COLS), NN)
            total = term if total is None else total + term
        return total

    psend[...] = project(o)
    send(psend, precv, r_p.at[0], mate)
    stream_s[...] = resid[...].astype(f32) + project(c)
    arrived(precv, r_p.at[0])
    stream = stream_s[...] + precv[...]
    stream_s[...] = stream

    gains = gain[...]
    raw = None
    for part in parts_of(stream * gains, 3):
        term = mul(heads_t[...], part, NT)
        raw = term if raw is None else raw + term
    square = None
    for part in parts_of(stream * stream, 3):
        term = mul(jnp.ones((16, COLS), bf16), part, NT)
        square = term if square is None else square + term
    raw_rows = lax.broadcasted_iota(i32, (RAW, ROWS), 0)
    rawbuf[x] = jnp.where(
        raw_rows == A + 1, jnp.broadcast_to(square[0:1], (RAW, ROWS)), raw[0:RAW]
    )
    for d in (2, 1, 3):
        send(rawbuf.at[x], rawbuf.at[x], r_raw.at[x], dev(d, 0, 0, c))
    for m in range(4):
        for zz in range(2):
            for cc in range(2):
                ctx_t[2 * m + zz, :, cc * ROWS : cc * ROWS + ROWS] = ctxbuf[m, cc, zz].T
    for d in (1, 3, 2):
        xx = (x + d) % 4
        arrived(rawbuf.at[xx], r_raw.at[xx])
    raw = ((rawbuf[0] + rawbuf[1]) + rawbuf[2]) + rawbuf[3]

    inverse = lax.rsqrt(jnp.broadcast_to(raw[A + 1 : A + 2], (8, ROWS)) / D + epsilon)
    out = raw * jnp.broadcast_to(inverse[0:1], (RAW, ROWS))
    values = jnp.broadcast_to(out[A : A + 1], (8, ROWS))

    def later(v, n):
        return pltpu.roll(v, ROWS - n, 1)

    last = step == STEPS - 1
    next_values = jnp.where(last, 0.0, later(values, 1))
    delta = reward + discount * keep * next_values - values
    adv = valid * delta
    factor = jnp.where(last, 0.0, valid * (discount * trace_decay) * keep)
    adv = adv + factor * later(adv, 1)
    factor = factor * later(factor, 1)
    adv = adv + factor * later(adv, 2)
    factor = factor * later(factor, 2)
    adv = adv + factor * later(adv, 4)

    adv32 = jnp.broadcast_to(adv[0:1], (32, ROWS))
    valid32 = jnp.broadcast_to(valid[0:1], (32, ROWS))
    sums = jnp.sum(jnp.where(learner_hit, adv32, 0.0), axis=1, keepdims=True)
    counts = jnp.sum(jnp.where(learner_hit, valid32, 0.0), axis=1, keepdims=True)
    lane128 = lax.broadcasted_iota(i32, (32, 128), 1)
    sub128 = lax.broadcasted_iota(i32, (32, 128), 0)
    at_sum = lane128 == sub128
    at_count = lane128 == sub128 + 32
    message = jnp.sum(
        jnp.where(at_sum, sums, 0.0) + jnp.where(at_count, counts, 0.0), axis=0, keepdims=True
    )
    l1[me16] = message
    lsrc[...] = message
    for d in FAR_FIRST:
        for core in range(2):
            send(lsrc, l1.at[me16], r_l1.at[me16], dev(0, 0, d, core))
    send(lsrc, l1.at[me16], r_l1.at[me16], mate)

    act_rows = raw_rows < A
    logits = jnp.where(act_rows, out, -1e30)
    top = jnp.max(logits, axis=0, keepdims=True)
    expo = jnp.where(act_rows, jnp.exp(logits - top), 0.0)
    prob = expo / jnp.sum(expo, axis=0, keepdims=True)
    chosen = raw_rows.astype(f32) == jnp.broadcast_to(action[0:1], (RAW, ROWS))
    score = prob - jnp.where(chosen, 1.0, 0.0)
    adv_grid = None
    for part in parts_of(jnp.where(own_step, adv, 0.0), 3):
        term = mul(part, env_b, NT)
        adv_grid = term if adv_grid is None else adv_grid + term
    adv_out[...] = adv_grid

    for s in range(1, 16):
        ss = (me16 + s) % 16
        arrived(l1.at[ss], r_l1.at[ss])
    total = l1[0]
    for s in range(1, 16):
        total = total + l1[s]
    l2[y] = total
    for d in FAR_FIRST:
        send(l2.at[y], l2.at[y], r_l2.at[y], dev(0, d, 0, c))
    for d in range(1, 8):
        yy = (y + d) % 8
        arrived(l2.at[yy], r_l2.at[yy])
    total = l2[0]
    for s in range(1, 8):
        total = total + l2[s]
    wide = jnp.broadcast_to(total, (32, 128))
    sums = jnp.sum(jnp.where(at_sum, wide, 0.0), axis=1, keepdims=True)
    counts = jnp.sum(jnp.where(at_count, wide, 0.0), axis=1, keepdims=True)
    means = sums / counts
    own = jnp.sum(jnp.where(sub128 == dp, means, 0.0), axis=0, keepdims=True)
    misc_out[...] = jnp.broadcast_to(own, (8, 128))

    mean_row = jnp.sum(jnp.where(learner_hit, means, 0.0), axis=0, keepdims=True)
    count_row = jnp.sum(jnp.where(learner_hit, counts, 0.0), axis=0, keepdims=True)
    weight = valid[0:1] / count_row
    centered = adv[0:1] - mean_row
    grad_value_row = -value_weight * weight * adv[0:1]
    grad_out = jnp.where(
        act_rows,
        (weight * centered) * score,
        jnp.where(raw_rows == A, jnp.broadcast_to(grad_value_row, (RAW, ROWS)), 0.0),
    )
    inner = jnp.sum(grad_out * raw, axis=0, keepdims=True)
    inv = inverse[0:1]
    coef = inv * inv * inv * inner / D
    scaled_out = grad_out * inv
    tall = jnp.concatenate([scaled_out, jnp.broadcast_to(coef, (HP - RAW, ROWS))], axis=0)
    tall_rows = lax.broadcasted_iota(i32, (HP, ROWS), 0)
    tall = jnp.where(tall_rows <= RAW, tall, 0.0)
    tall_parts = parts_of(tall, 2)

    one_row = (lax.broadcasted_iota(i32, (HP, 128), 0) == RAW).astype(f32).astype(bf16)
    grad_normed = mul(tall_parts[0], heads_t[...], TN) + mul(tall_parts[1], heads_t[...], TN)
    coef_col = mul(tall_parts[0], one_row, TN) + mul(tall_parts[1], one_row, TN)
    stream = stream_s[...]
    coef_wide = jnp.concatenate([coef_col] * 4, axis=1)
    gstream[c] = (gains * grad_normed - stream * coef_wide).astype(bf16)
    send(gstream.at[c], gstream.at[c], r_g.at[0], mate)

    high, low = parts_of(stream, 2)
    q = mul(tall_parts[0], high, NN) + mul(tall_parts[0], low, NN) + mul(tall_parts[1], high, NN)
    for p in range(16):
        qsrc[p % 2, p // 2] = q[
            (p % 4) * 16 : (p % 4) * 16 + 16, (p // 4) * 128 : (p // 4) * 128 + 128
        ]
    send(qsrc.at[o], qmate, r_q0.at[0], mate)

    arrived(qmate, r_q0.at[0])
    qsum[...] = qsrc[c] + qmate[...]
    q1[z] = qsum[z]
    for d in FAR_FIRST:
        zz = (z + d) % 8
        send(qsum.at[zz], q1.at[z], r_q1.at[z], dev(0, 0, d, c))

    arrived(gstream.at[o], r_g.at[0])
    first_cols, last_cols = pl.ds(0, HALF), pl.ds(HALF, HALF)
    grads = gstream[...].reshape(2 * ROWS, COLS)
    for d in FAR_FIRST + (0,):
        zz = (z + d) % 8
        block = mul(ctx_t[zz], grads, NN).astype(bf16).reshape(2, 4, 16, COLS)
        pb[zz] = block
        if d:
            send(pb.at[zz, :, :, :, first_cols], ra.at[z], r_ra.at[z], dev(0, 0, d, c))
        else:
            ra[z] = block[:, :, :, 0:HALF]

    def gather_sum(buf, sems, own, wait_own):
        if wait_own:
            arrived(buf.at[own], sems.at[own])
        total = buf[own].astype(f32)
        for d in (1, 7, 2, 6, 3, 5, 4):
            n = (own + d) % 8
            arrived(buf.at[n], sems.at[n])
            total = total + buf[n].astype(f32)
        return total

    def to_half(rr, core):
        here = jnp.logical_and(jnp.logical_and(h == c, r == rr), c == core)
        return here, {"role": rr, "dp": z * 4 + c * 2 + core, "mp": x}

    for core in range(2):
        for rr in range(4):
            here, device = to_half(rr, core)
            send_or_keep(here, pb.at[:, core, rr, :, last_cols], rb.at[y], r_rb.at[y], device)

    for d in range(1, 8):
        zz = (z + d) % 8
        arrived(q1.at[zz], r_q1.at[zz])
    total = q1[0]
    for s in range(1, 8):
        total = total + q1[s]
    q2[y] = total
    for d in FAR_FIRST:
        send(q2.at[y], q2.at[y], r_q2.at[y], dev(0, d, 0, c))

    sa2[...] = gather_sum(ra, r_ra, z, False)
    for core in range(2):
        for rr in range(4):
            here, device = to_half(rr, core)
            send_or_keep(here, sa2.at[core, rr], ra2.at[y], r_ra2.at[y], device)
    sb2[...] = gather_sum(rb, r_rb, y, True)
    rb2[z] = sb2[z]
    for d in FAR_FIRST:
        send(sb2.at[(z + d) % 8], rb2.at[z], r_rb2.at[z], dev(0, 0, d, c))

    for d in range(1, 8):
        yy = (y + d) % 8
        arrived(q2.at[yy], r_q2.at[yy])
    total = q2[0]
    for s in range(1, 8):
        total = total + q2[s]
    qf[c, z] = total
    for d in FAR_FIRST:
        send(qf.at[c, z], qf.at[c, z], r_q3.at[z], dev(0, 0, d, c))

    def to_roles(part, cols):
        for d in (2, 1, 3):
            device = {"role": (r + d) % 4, "dp": dp, "mp": x}
            block = gw_out.at[r, :, cols]
            send(block, block, r_f.at[part * 4 + r], device)

    gw_out[r, :, 0:HALF] = gather_sum(ra2, r_ra2, y, True)
    to_roles(0, first_cols)
    gw_out[r, :, HALF:] = gather_sum(rb2, r_rb2, z, False)
    to_roles(1, last_cols)

    for d in range(1, 8):
        zz = (z + d) % 8
        arrived(qf.at[c, zz], r_q3.at[zz])
    send(qf.at[c], qf.at[c], r_q4.at[0], mate)
    arrived(qf.at[o], r_q4.at[0])
    rows = lax.broadcasted_iota(i32, (RAW, 128), 0)
    for lane in range(4):
        cols = slice(lane * 128, lane * 128 + 128)
        block = jnp.concatenate([qf[s % 2, lane * 2 + s // 2] for s in range(3)], axis=0)
        gain_row = jnp.sum(block * heads_t[0:RAW, cols].astype(f32), axis=0, keepdims=True)
        heads_out[:, cols] = jnp.where(
            rows == A + 1, jnp.broadcast_to(gain_row, (RAW, 128)), block * gains[:, cols]
        )

    for d in range(1, 4):
        rr = (r + d) % 4
        arrived(gw_out.at[rr, :, first_cols], r_f.at[rr])
        arrived(gw_out.at[rr, :, last_cols], r_f.at[4 + rr])

    for condition, copy in pending:
        if condition is None:
            copy.wait_send()
        else:
            pl.when(condition)(copy.wait_send)


def finish(adv, misc, gw, heads, adv_o, mean_o, gw_o, gain_o, policy_o, value_o):
    adv_o[...] = adv[...]
    mean_o[...] = misc[0:1, 0:1]
    gw_o[...] = gw[...].reshape(64, COLS)
    gain_o[...] = heads[A + 1 : A + 2]
    policy_o[...] = heads[0:A]
    value_o[...] = heads[A : A + 1]


def per_device(
    residual_in,
    context,
    w_out,
    norm_gain,
    policy_head,
    value_head,
    rewards,
    resets,
    actions,
    lengths,
    assignment,
):
    vmem = pl.BlockSpec(memory_space=pltpu.VMEM)
    hbm = pl.BlockSpec(memory_space=pltpu.HBM)
    dma = pltpu.SemaphoreType.DMA
    buffers = [
        pltpu.VMEM((ROWS, COLS), bf16),
        pltpu.VMEM((1, COLS), f32),
        pltpu.VMEM((A, COLS), bf16),
        pltpu.VMEM((COLS,), bf16),
        pltpu.VMEM((STEPS, 32), bf16),
        pltpu.VMEM((STEPS, 32), i32),
        pltpu.VMEM((STEPS, 32), i32),
        pltpu.VMEM((1, 32), i32),
        pltpu.VMEM((1, 32), i32),
        pltpu.VMEM((4, 2, 2, ROWS, 128), bf16),
        pltpu.VMEM((8, 128, 2 * ROWS), bf16),
        pltpu.VMEM((8, 2, 4, 16, COLS), bf16),
        pltpu.VMEM((ROWS, COLS), f32),
        pltpu.VMEM((ROWS, COLS), f32),
        pltpu.VMEM((ROWS, COLS), f32),
        pltpu.VMEM((2, ROWS, COLS), bf16),
        pltpu.VMEM((4, RAW, ROWS), f32),
        pltpu.VMEM((16, 1, 128), f32),
        pltpu.VMEM((8, 1, 128), f32),
        pltpu.VMEM((1, 128), f32),
        pltpu.VMEM((HP, COLS), bf16),
        pltpu.VMEM((2, 8, 16, 128), f32),
        pltpu.VMEM((8, 16, 128), f32),
        pltpu.VMEM((8, 16, 128), f32),
        pltpu.VMEM((8, 16, 128), f32),
        pltpu.VMEM((8, 16, 128), f32),
        pltpu.VMEM((2, 8, 16, 128), f32),
        pltpu.VMEM((8, 2, 4, 16, COLS), bf16),
        pltpu.VMEM((8, 2, 4, 16, HALF), bf16),
        pltpu.VMEM((8, 8, 16, HALF), bf16),
        pltpu.VMEM((2, 4, 16, HALF), f32),
        pltpu.VMEM((8, 16, HALF), f32),
        pltpu.VMEM((8, 16, HALF), f32),
        pltpu.VMEM((8, 16, HALF), f32),
    ]
    counts = [160, 9, 16, 16, 16, 1, 4, 16, 8, 1, 1, 8, 8, 8, 1, 8, 8, 8, 8, 8]
    step_out = pl.pallas_call(
        kernel,
        out_shape=(
            jax.ShapeDtypeStruct((STEPS, 32), f32),
            jax.ShapeDtypeStruct((8, 128), f32),
            jax.ShapeDtypeStruct((4, 16, COLS), f32),
            jax.ShapeDtypeStruct((RAW, COLS), f32),
        ),
        in_specs=[hbm] * 11,
        out_specs=(vmem,) * 4,
        scratch_shapes=buffers
        + [dma((n,)) for n in counts]
        + [pltpu.SemaphoreType.REGULAR((6,))],
        compiler_params=pltpu.CompilerParams(
            collective_id=0, has_side_effects=True, vmem_limit_bytes=62 * 1024 * 1024
        ),
        name="policy_step",
    )(
        residual_in.reshape(ROWS, COLS),
        context.reshape(ROWS, COLS),
        w_out.reshape(4, 16, COLS),
        norm_gain.reshape(1, COLS),
        policy_head.T,
        value_head,
        rewards.T,
        resets.T,
        actions.T,
        lengths.reshape(1, 32),
        assignment.reshape(1, 32),
    )
    adv, mean, grad_w, grad_gain, grad_policy, grad_value = pl.pallas_call(
        finish,
        out_shape=(
            jax.ShapeDtypeStruct((STEPS, 32), f32),
            jax.ShapeDtypeStruct((1, 1), f32),
            jax.ShapeDtypeStruct((64, COLS), f32),
            jax.ShapeDtypeStruct((1, COLS), f32),
            jax.ShapeDtypeStruct((A, COLS), f32),
            jax.ShapeDtypeStruct((1, COLS), f32),
        ),
        in_specs=[vmem] * 4,
        out_specs=(vmem,) * 6,
        name="write_outputs",
    )(*step_out)
    return (
        adv.T,
        mean.reshape(1),
        grad_w,
        grad_gain.reshape(COLS),
        grad_policy.T,
        grad_value.reshape(COLS),
    )


def solution(mesh):
    placed = (
        P(("role", "dp"), None, "mp"),
        P(("role", "dp"), None, "mp"),
        P("dp", "mp"),
        P("mp"),
        P("mp", None),
        P("mp"),
        P(("role", "dp"), None),
        P(("role", "dp"), None),
        P(("role", "dp"), None),
        P(("role", "dp")),
        P(("role", "dp")),
    )
    return jax.shard_map(
        per_device,
        mesh=mesh,
        in_specs=placed,
        out_specs=(
            P(("role", "dp"), None),
            P("dp"),
            P("dp", "mp"),
            P("mp"),
            P("mp", None),
            P("mp"),
        ),
        check_vma=False,
    )
```

```python
import jax
import jax.numpy as jnp
from jax import lax
from jax.experimental import pallas as pl
from jax.experimental.pallas import tpu as pltpu
from jax.sharding import PartitionSpec as P

D = 2048
A = 43
STEPS = 8
ROWS = 256
COLS = 512
HALF = 256
HP = 64
RAW = 48

discount = 0.99
trace_decay = 0.95
value_weight = 0.5
epsilon = 1e-05

MESH = pl.DeviceIdType.MESH
bf16 = jnp.bfloat16
f32 = jnp.float32
i32 = jnp.int32

NN = (((1,), (0,)), ((), ()))
NT = (((1,), (1,)), ((), ()))
TN = (((0,), (0,)), ((), ()))


def mul(a, b, dims):
    return lax.dot_general(a, b, dims, preferred_element_type=f32)


def parts_of(a, n):
    out = []
    for _ in range(n):
        high = a.astype(bf16)
        out.append(high)
        a = a - high.astype(f32)
    return out


FAR_FIRST = (4, 3, 5, 2, 6, 1, 7)


def kernel(
    resid_h, ctx_h, w_h, gain_h, policy_h, value_h,
    rewards_h, resets_h, actions_h, lengths_h, assign_h,
    adv_out, misc_out, gw_out, heads_out,
    resid, gain, policy, value, rewards, resets, actions, lengths, assign,
    ctxbuf, ctx_t, wbuf, psend, precv, stream_s, gstream,
    rawbuf, l1, l2, lsrc, heads_t, qsrc, qmate, qsum, q1, q2, qf,
    pb, ra, rb, sa2, sb2, ra2, rb2,
    s_all, r_in, r_ctx, r_w, r_wy, r_p, r_raw, r_l1, r_l2, r_g,
    r_q0, r_q1, r_q2, r_q3, r_q4, r_ra, r_rb, r_ra2, r_rb2, r_f, tokens,
):
    role = lax.axis_index("role")
    dp = lax.axis_index("dp")
    x = lax.axis_index("mp")
    z = dp // 4
    h = (dp // 2) % 2
    c = dp % 2
    y = h * 4 + role
    r = role
    o = 1 - c
    me16 = z * 2 + c

    def dev(dx, dy, dz, core):
        yy = (y + dy + 8) % 8
        return {
            "role": yy % 4,
            "dp": ((z + dz + 8) % 8) * 4 + (yy // 4) * 2 + core,
            "mp": (x + dx + 4) % 4,
        }

    mate = dev(0, 0, 0, o)
    pending = []

    def remote(src, dst, rsem, device):
        slot = len(pending)
        return pltpu.make_async_remote_copy(
            src_ref=src,
            dst_ref=dst,
            send_sem=s_all.at[slot],
            recv_sem=rsem,
            device_id=device,
            device_id_type=MESH,
        )

    def send(src, dst, rsem, device):
        copy = remote(src, dst, rsem, device)
        copy.start()
        pending.append((None, copy))

    def send_when(condition, src, dst, rsem, device):
        copy = remote(src, dst, rsem, device)
        pl.when(condition)(copy.start)
        pending.append((condition, copy))

    def send_or_keep(here, src, dst, rsem, device):
        copy = remote(src, dst, rsem, device)
        away = jnp.logical_not(here)

        @pl.when(here)
        def _():
            pltpu.make_async_copy(src, dst, rsem).start()

        @pl.when(away)
        def _():
            copy.start()

        pending.append((away, copy))

    def arrived(dst, rsem):
        pltpu.make_async_copy(dst, dst, rsem).wait()

    small = [
        (gain_h, gain), (policy_h, policy), (value_h, value), (rewards_h, rewards),
        (resets_h, resets), (actions_h, actions), (lengths_h, lengths), (assign_h, assign),
        (resid_h, resid),
    ]
    for n, (src, dst) in enumerate(small):
        pltpu.make_async_copy(src, dst, r_in.at[n]).start()

    barrier = pltpu.get_barrier_semaphore()
    peers = [mate, dev(1, 0, 0, 0), dev(1, 0, 0, 1), dev(3, 0, 0, 0), dev(3, 0, 0, 1)]
    peers += [dev(0, 0, d, c) for d in (1, 2, 6, 7)]
    peers += [dev(0, 1, 0, c), dev(0, 7, 0, c)]
    source = 3 * (1 - r // 2)
    peers += [{"role": source, "dp": z * 4 + (1 - h) * 2 + core, "mp": x} for core in range(2)]
    border = r % 3 == 0
    for peer in peers:
        pl.semaphore_signal(barrier, inc=1, device_id=peer, device_id_type=MESH)
    pl.semaphore_wait(barrier, len(peers) - 2 + jnp.where(border, 4, 0))

    def tell(n):
        pl.semaphore_signal(tokens.at[2 * n], inc=1, device_id=dev(0, 1, 0, c), device_id_type=MESH)
        pl.semaphore_signal(
            tokens.at[2 * n + 1], inc=1, device_id=dev(0, 7, 0, c), device_id_type=MESH
        )

    def hear(n):
        pl.semaphore_wait(tokens.at[2 * n], 1)
        pl.semaphore_wait(tokens.at[2 * n + 1], 1)

    tell(0)

    mine = pl.ds(pl.multiple_of((y % 2) * HALF, HALF), HALF)
    theirs = pl.ds(pl.multiple_of((1 - y % 2) * HALF, HALF), HALF)
    for n in range(2):
        to_role = jnp.where(r == 3, n, 3 - n)
        cols = pl.ds(pl.multiple_of((to_role % 2) * HALF, HALF), HALF)
        across = {"role": to_role, "dp": z * 4 + (1 - h) * 2 + h, "mp": x}
        send_when(
            border, w_h.at[:, :, cols], wbuf.at[z, c, :, :, cols], r_w.at[z * 2 + c], across
        )
    send_or_keep(
        c == h, w_h.at[:, :, mine], wbuf.at[z, c, :, :, mine], r_w.at[z * 2 + c], mate
    )

    def piece(zz, core):
        return ctx_h.at[:, pl.ds(pl.multiple_of(zz * 256 + core * 128, 128), 128)]

    def ctx_sem(m, cc, zz):
        return r_ctx.at[(m * 2 + cc) * 2 + zz]

    for first in range(2):
        for dx, zz in ((1, first), (3, 1 - first)):
            for core in range(2):
                send(piece(zz, core), ctxbuf.at[x, c, zz], ctx_sem(x, c, zz), dev(dx, 0, 0, core))
    for zz in range(2):
        pltpu.make_async_copy(piece(zz, c), ctxbuf.at[x, c, zz], ctx_sem(x, c, zz)).start()
        send(piece(zz, o), ctxbuf.at[x, c, zz], ctx_sem(x, c, zz), mate)

    def w_block(zz, cc):
        return wbuf.at[zz, cc, :, :, mine], r_w.at[zz * 2 + cc]

    def to_y(zz, cc):
        block = wbuf.at[zz, cc, :, :, mine]
        send(block, block, r_wy.at[zz * 2 + cc], dev(0, 1 if cc == 0 else 7, 0, c))

    for cc in range(2):
        block, sem = w_block(z, cc)
        arrived(block, sem)
        for d in (2, 6, 1, 7):
            send(block, block, sem, dev(0, 0, d, c))
        to_y(z, cc)

    for n in range(9):
        pltpu.make_async_copy(small[n][0], small[n][1], r_in.at[n]).wait()
    lane8 = lax.broadcasted_iota(i32, (8, ROWS), 1)
    sub8 = lax.broadcasted_iota(i32, (8, ROWS), 0)
    step = lane8 % STEPS
    own_step = step == sub8
    lane32 = lax.broadcasted_iota(i32, (32, ROWS), 1)
    sub32 = lax.broadcasted_iota(i32, (32, ROWS), 0)
    env_b = (lane32 // STEPS == sub32).astype(f32).astype(bf16)

    def to_row(grid):
        wide = jnp.where(own_step, mul(grid.astype(f32).astype(bf16), env_b, NN), 0.0)
        return jnp.broadcast_to(jnp.sum(wide, axis=0, keepdims=True), (8, ROWS))

    def env_row(vector):
        return mul(jnp.broadcast_to(vector.astype(f32), (8, 32)).astype(bf16), env_b, NN)

    reward = to_row(rewards[...])
    keep = 1.0 - to_row(resets[...])
    action = to_row(actions[...])
    length = env_row(lengths[...])
    learner = env_row(assign[...])
    valid = (step.astype(f32) < length).astype(f32)
    learner_hit = jnp.broadcast_to(learner[0:1], (32, ROWS)) == sub32.astype(f32)
    head_rows = lax.broadcasted_iota(i32, (HP, COLS), 0)
    heads_t[...] = jnp.where(
        head_rows == A,
        jnp.broadcast_to(value[...].astype(f32).reshape(1, COLS), (HP, COLS)),
        jnp.concatenate([policy[...].astype(f32), jnp.zeros((HP - A, COLS), f32)], axis=0),
    ).astype(bf16)

    for m, zz, dx in (((x + 3) % 4, 0, 1), ((x + 1) % 4, 1, 3)):
        for cc in range(2):
            block = ctxbuf.at[m, cc, zz]
            arrived(block, ctx_sem(m, cc, zz))
            send(block, block, ctx_sem(m, cc, zz), dev(dx, 0, 0, c))

    hear(0)
    tell(1)
    for cc in range(2):
        for d in (6, 2):
            block, sem = w_block((z + d) % 8, cc)
            arrived(block, sem)
            if d == 6:
                if cc == 0:
                    send(block, block, sem, dev(0, 0, 2, c))
                send(block, block, sem, dev(0, 0, 1, c))
            else:
                if cc == 1:
                    send(block, block, sem, dev(0, 0, 6, c))
                send(block, block, sem, dev(0, 0, 7, c))
            to_y((z + d) % 8, cc)
    hear(1)
    tell(2)
    for d in (1, 7, 3, 5, 4):
        for cc in range(2):
            arrived(*w_block((z + d) % 8, cc))
            to_y((z + d) % 8, cc)

    for cc in range(2):
        for zz in range(2):
            arrived(ctxbuf.at[x, cc, zz], ctx_sem(x, cc, zz))
            m = (x + 2) % 4
            arrived(ctxbuf.at[m, cc, zz], ctx_sem(m, cc, zz))
        m = (x + 3) % 4
        arrived(ctxbuf.at[m, cc, 1], ctx_sem(m, cc, 1))
        m = (x + 1) % 4
        arrived(ctxbuf.at[m, cc, 0], ctx_sem(m, cc, 0))
    hear(2)
    for s in range(8):
        for cc in range(2):
            arrived(wbuf.at[s, cc, :, :, theirs], r_wy.at[s * 2 + cc])

    def project(core):
        total = None
        for m in range(4):
            left = jnp.concatenate([ctxbuf[m, core, 0], ctxbuf[m, core, 1]], axis=1)
            term = mul(left, wbuf[2 * m : 2 * m + 2].reshape(256, COLS), NN)
            total = term if total is None else total + term
        return total

    psend[...] = project(o)
    send(psend, precv, r_p.at[0], mate)
    stream_s[...] = resid[...].astype(f32) + project(c)
    arrived(precv, r_p.at[0])
    stream = stream_s[...] + precv[...]
    stream_s[...] = stream

    gains = gain[...]
    raw = None
    for part in parts_of(stream * gains, 3):
        term = mul(heads_t[...], part, NT)
        raw = term if raw is None else raw + term
    square = None
    for part in parts_of(stream * stream, 3):
        term = mul(jnp.ones((16, COLS), bf16), part, NT)
        square = term if square is None else square + term
    raw_rows = lax.broadcasted_iota(i32, (RAW, ROWS), 0)
    rawbuf[x] = jnp.where(
        raw_rows == A + 1, jnp.broadcast_to(square[0:1], (RAW, ROWS)), raw[0:RAW]
    )
    for d in (2, 1, 3):
        send(rawbuf.at[x], rawbuf.at[x], r_raw.at[x], dev(d, 0, 0, c))
    for m in range(4):
        for zz in range(2):
            for cc in range(2):
                ctx_t[2 * m + zz, :, cc * ROWS : cc * ROWS + ROWS] = ctxbuf[m, cc, zz].T
    for d in (1, 3, 2):
        xx = (x + d) % 4
        arrived(rawbuf.at[xx], r_raw.at[xx])
    raw = ((rawbuf[0] + rawbuf[1]) + rawbuf[2]) + rawbuf[3]

    inverse = lax.rsqrt(jnp.broadcast_to(raw[A + 1 : A + 2], (8, ROWS)) / D + epsilon)
    out = raw * jnp.broadcast_to(inverse[0:1], (RAW, ROWS))
    values = jnp.broadcast_to(out[A : A + 1], (8, ROWS))

    def later(v, n):
        return pltpu.roll(v, ROWS - n, 1)

    last = step == STEPS - 1
    next_values = jnp.where(last, 0.0, later(values, 1))
    delta = reward + discount * keep * next_values - values
    adv = valid * delta
    factor = jnp.where(last, 0.0, valid * (discount * trace_decay) * keep)
    adv = adv + factor * later(adv, 1)
    factor = factor * later(factor, 1)
    adv = adv + factor * later(adv, 2)
    factor = factor * later(factor, 2)
    adv = adv + factor * later(adv, 4)

    adv32 = jnp.broadcast_to(adv[0:1], (32, ROWS))
    valid32 = jnp.broadcast_to(valid[0:1], (32, ROWS))
    sums = jnp.sum(jnp.where(learner_hit, adv32, 0.0), axis=1, keepdims=True)
    counts = jnp.sum(jnp.where(learner_hit, valid32, 0.0), axis=1, keepdims=True)
    lane128 = lax.broadcasted_iota(i32, (32, 128), 1)
    sub128 = lax.broadcasted_iota(i32, (32, 128), 0)
    at_sum = lane128 == sub128
    at_count = lane128 == sub128 + 32
    message = jnp.sum(
        jnp.where(at_sum, sums, 0.0) + jnp.where(at_count, counts, 0.0), axis=0, keepdims=True
    )
    l1[me16] = message
    lsrc[...] = message
    for d in FAR_FIRST:
        for core in range(2):
            send(lsrc, l1.at[me16], r_l1.at[me16], dev(0, 0, d, core))
    send(lsrc, l1.at[me16], r_l1.at[me16], mate)

    act_rows = raw_rows < A
    logits = jnp.where(act_rows, out, -1e30)
    top = jnp.max(logits, axis=0, keepdims=True)
    expo = jnp.where(act_rows, jnp.exp(logits - top), 0.0)
    prob = expo / jnp.sum(expo, axis=0, keepdims=True)
    chosen = raw_rows.astype(f32) == jnp.broadcast_to(action[0:1], (RAW, ROWS))
    score = prob - jnp.where(chosen, 1.0, 0.0)
    adv_grid = None
    for part in parts_of(jnp.where(own_step, adv, 0.0), 3):
        term = mul(part, env_b, NT)
        adv_grid = term if adv_grid is None else adv_grid + term
    adv_out[...] = adv_grid

    for s in range(1, 16):
        ss = (me16 + s) % 16
        arrived(l1.at[ss], r_l1.at[ss])
    total = l1[0]
    for s in range(1, 16):
        total = total + l1[s]
    l2[y] = total
    for d in FAR_FIRST:
        send(l2.at[y], l2.at[y], r_l2.at[y], dev(0, d, 0, c))
    for d in range(1, 8):
        yy = (y + d) % 8
        arrived(l2.at[yy], r_l2.at[yy])
    total = l2[0]
    for s in range(1, 8):
        total = total + l2[s]
    wide = jnp.broadcast_to(total, (32, 128))
    sums = jnp.sum(jnp.where(at_sum, wide, 0.0), axis=1, keepdims=True)
    counts = jnp.sum(jnp.where(at_count, wide, 0.0), axis=1, keepdims=True)
    means = sums / counts
    own = jnp.sum(jnp.where(sub128 == dp, means, 0.0), axis=0, keepdims=True)
    misc_out[...] = jnp.broadcast_to(own, (8, 128))

    mean_row = jnp.sum(jnp.where(learner_hit, means, 0.0), axis=0, keepdims=True)
    count_row = jnp.sum(jnp.where(learner_hit, counts, 0.0), axis=0, keepdims=True)
    weight = valid[0:1] / count_row
    centered = adv[0:1] - mean_row
    grad_value_row = -value_weight * weight * adv[0:1]
    grad_out = jnp.where(
        act_rows,
        (weight * centered) * score,
        jnp.where(raw_rows == A, jnp.broadcast_to(grad_value_row, (RAW, ROWS)), 0.0),
    )
    inner = jnp.sum(grad_out * raw, axis=0, keepdims=True)
    inv = inverse[0:1]
    coef = inv * inv * inv * inner / D
    scaled_out = grad_out * inv
    tall = jnp.concatenate([scaled_out, jnp.broadcast_to(coef, (HP - RAW, ROWS))], axis=0)
    tall_rows = lax.broadcasted_iota(i32, (HP, ROWS), 0)
    tall = jnp.where(tall_rows <= RAW, tall, 0.0)
    tall_parts = parts_of(tall, 2)

    one_row = (lax.broadcasted_iota(i32, (HP, 128), 0) == RAW).astype(f32).astype(bf16)
    grad_normed = mul(tall_parts[0], heads_t[...], TN) + mul(tall_parts[1], heads_t[...], TN)
    coef_col = mul(tall_parts[0], one_row, TN) + mul(tall_parts[1], one_row, TN)
    stream = stream_s[...]
    coef_wide = jnp.concatenate([coef_col] * 4, axis=1)
    gstream[c] = (gains * grad_normed - stream * coef_wide).astype(bf16)
    send(gstream.at[c], gstream.at[c], r_g.at[0], mate)

    high, low = parts_of(stream, 2)
    q = mul(tall_parts[0], high, NN) + mul(tall_parts[0], low, NN) + mul(tall_parts[1], high, NN)
    for p in range(16):
        qsrc[p % 2, p // 2] = q[
            (p % 4) * 16 : (p % 4) * 16 + 16, (p // 4) * 128 : (p // 4) * 128 + 128
        ]
    send(qsrc.at[o], qmate, r_q0.at[0], mate)

    arrived(qmate, r_q0.at[0])
    qsum[...] = qsrc[c] + qmate[...]
    q1[z] = qsum[z]
    for d in FAR_FIRST:
        zz = (z + d) % 8
        send(qsum.at[zz], q1.at[z], r_q1.at[z], dev(0, 0, d, c))

    arrived(gstream.at[o], r_g.at[0])
    first_cols, last_cols = pl.ds(0, HALF), pl.ds(HALF, HALF)
    grads = gstream[...].reshape(2 * ROWS, COLS)
    for d in FAR_FIRST + (0,):
        zz = (z + d) % 8
        block = mul(ctx_t[zz], grads, NN).astype(bf16).reshape(2, 4, 16, COLS)
        pb[zz] = block
        if d:
            send(pb.at[zz, :, :, :, first_cols], ra.at[z], r_ra.at[z], dev(0, 0, d, c))
        else:
            ra[z] = block[:, :, :, 0:HALF]

    def gather_sum(buf, sems, own, wait_own):
        if wait_own:
            arrived(buf.at[own], sems.at[own])
        total = buf[own].astype(f32)
        for d in (1, 7, 2, 6, 3, 5, 4):
            n = (own + d) % 8
            arrived(buf.at[n], sems.at[n])
            total = total + buf[n].astype(f32)
        return total

    def to_half(block_of, dst, rsem):
        for n in (2, 1, 3, 0):
            rr = (r + n) % 4
            for core in range(2):
                block = block_of(core, rr)
                device = {"role": rr, "dp": z * 4 + c * 2 + core, "mp": x}
                if n:
                    send(block, dst, rsem, device)
                else:
                    here = jnp.logical_and(h == c, c == core)
                    send_or_keep(here, block, dst, rsem, device)

    to_half(lambda core, rr: pb.at[:, core, rr, :, last_cols], rb.at[y], r_rb.at[y])

    for d in range(1, 8):
        zz = (z + d) % 8
        arrived(q1.at[zz], r_q1.at[zz])
    total = q1[0]
    for s in range(1, 8):
        total = total + q1[s]
    q2[y] = total
    for d in FAR_FIRST:
        send(q2.at[y], q2.at[y], r_q2.at[y], dev(0, d, 0, c))

    sa2[...] = gather_sum(ra, r_ra, z, False)
    to_half(lambda core, rr: sa2.at[core, rr], ra2.at[y], r_ra2.at[y])
    sb2[...] = gather_sum(rb, r_rb, y, True)
    rb2[z] = sb2[z]
    for d in FAR_FIRST:
        send(sb2.at[(z + d) % 8], rb2.at[z], r_rb2.at[z], dev(0, 0, d, c))

    for d in range(1, 8):
        yy = (y + d) % 8
        arrived(q2.at[yy], r_q2.at[yy])
    total = q2[0]
    for s in range(1, 8):
        total = total + q2[s]
    qf[c, z] = total
    for d in FAR_FIRST:
        send(qf.at[c, z], qf.at[c, z], r_q3.at[z], dev(0, 0, d, c))

    def to_roles(part, cols):
        for d in (2, 1, 3):
            device = {"role": (r + d) % 4, "dp": dp, "mp": x}
            block = gw_out.at[r, :, cols]
            send(block, block, r_f.at[part * 4 + r], device)

    gw_out[r, :, 0:HALF] = gather_sum(ra2, r_ra2, y, True)
    to_roles(0, first_cols)
    gw_out[r, :, HALF:] = gather_sum(rb2, r_rb2, z, False)
    to_roles(1, last_cols)

    for d in range(1, 8):
        zz = (z + d) % 8
        arrived(qf.at[c, zz], r_q3.at[zz])
    send(qf.at[c], qf.at[c], r_q4.at[0], mate)
    arrived(qf.at[o], r_q4.at[0])
    rows = lax.broadcasted_iota(i32, (RAW, 128), 0)
    for lane in range(4):
        cols = slice(lane * 128, lane * 128 + 128)
        block = jnp.concatenate([qf[s % 2, lane * 2 + s // 2] for s in range(3)], axis=0)
        gain_row = jnp.sum(block * heads_t[0:RAW, cols].astype(f32), axis=0, keepdims=True)
        heads_out[:, cols] = jnp.where(
            rows == A + 1, jnp.broadcast_to(gain_row, (RAW, 128)), block * gains[:, cols]
        )

    for d in range(1, 4):
        rr = (r + d) % 4
        arrived(gw_out.at[rr, :, first_cols], r_f.at[rr])
        arrived(gw_out.at[rr, :, last_cols], r_f.at[4 + rr])

    for condition, copy in pending:
        if condition is None:
            copy.wait_send()
        else:
            pl.when(condition)(copy.wait_send)


def finish(adv, misc, gw, heads, adv_o, mean_o, gw_o, gain_o, policy_o, value_o):
    adv_o[...] = adv[...]
    mean_o[...] = misc[0:1, 0:1]
    gw_o[...] = gw[...].reshape(64, COLS)
    gain_o[...] = heads[A + 1 : A + 2]
    policy_o[...] = heads[0:A]
    value_o[...] = heads[A : A + 1]


def per_device(
    residual_in,
    context,
    w_out,
    norm_gain,
    policy_head,
    value_head,
    rewards,
    resets,
    actions,
    lengths,
    assignment,
):
    vmem = pl.BlockSpec(memory_space=pltpu.VMEM)
    hbm = pl.BlockSpec(memory_space=pltpu.HBM)
    dma = pltpu.SemaphoreType.DMA
    buffers = [
        pltpu.VMEM((ROWS, COLS), bf16),
        pltpu.VMEM((1, COLS), f32),
        pltpu.VMEM((A, COLS), bf16),
        pltpu.VMEM((COLS,), bf16),
        pltpu.VMEM((STEPS, 32), bf16),
        pltpu.VMEM((STEPS, 32), i32),
        pltpu.VMEM((STEPS, 32), i32),
        pltpu.VMEM((1, 32), i32),
        pltpu.VMEM((1, 32), i32),
        pltpu.VMEM((4, 2, 2, ROWS, 128), bf16),
        pltpu.VMEM((8, 128, 2 * ROWS), bf16),
        pltpu.VMEM((8, 2, 4, 16, COLS), bf16),
        pltpu.VMEM((ROWS, COLS), f32),
        pltpu.VMEM((ROWS, COLS), f32),
        pltpu.VMEM((ROWS, COLS), f32),
        pltpu.VMEM((2, ROWS, COLS), bf16),
        pltpu.VMEM((4, RAW, ROWS), f32),
        pltpu.VMEM((16, 1, 128), f32),
        pltpu.VMEM((8, 1, 128), f32),
        pltpu.VMEM((1, 128), f32),
        pltpu.VMEM((HP, COLS), bf16),
        pltpu.VMEM((2, 8, 16, 128), f32),
        pltpu.VMEM((8, 16, 128), f32),
        pltpu.VMEM((8, 16, 128), f32),
        pltpu.VMEM((8, 16, 128), f32),
        pltpu.VMEM((8, 16, 128), f32),
        pltpu.VMEM((2, 8, 16, 128), f32),
        pltpu.VMEM((8, 2, 4, 16, COLS), bf16),
        pltpu.VMEM((8, 2, 4, 16, HALF), bf16),
        pltpu.VMEM((8, 8, 16, HALF), bf16),
        pltpu.VMEM((2, 4, 16, HALF), f32),
        pltpu.VMEM((8, 16, HALF), f32),
        pltpu.VMEM((8, 16, HALF), f32),
        pltpu.VMEM((8, 16, HALF), f32),
    ]
    counts = [160, 9, 16, 16, 16, 1, 4, 16, 8, 1, 1, 8, 8, 8, 1, 8, 8, 8, 8, 8]
    step_out = pl.pallas_call(
        kernel,
        out_shape=(
            jax.ShapeDtypeStruct((STEPS, 32), f32),
            jax.ShapeDtypeStruct((8, 128), f32),
            jax.ShapeDtypeStruct((4, 16, COLS), f32),
            jax.ShapeDtypeStruct((RAW, COLS), f32),
        ),
        in_specs=[hbm] * 11,
        out_specs=(vmem,) * 4,
        scratch_shapes=buffers
        + [dma((n,)) for n in counts]
        + [pltpu.SemaphoreType.REGULAR((6,))],
        compiler_params=pltpu.CompilerParams(
            collective_id=0, has_side_effects=True, vmem_limit_bytes=62 * 1024 * 1024
        ),
        name="policy_step",
    )(
        residual_in.reshape(ROWS, COLS),
        context.reshape(ROWS, COLS),
        w_out.reshape(4, 16, COLS),
        norm_gain.reshape(1, COLS),
        policy_head.T,
        value_head,
        rewards.T,
        resets.T,
        actions.T,
        lengths.reshape(1, 32),
        assignment.reshape(1, 32),
    )
    adv, mean, grad_w, grad_gain, grad_policy, grad_value = pl.pallas_call(
        finish,
        out_shape=(
            jax.ShapeDtypeStruct((STEPS, 32), f32),
            jax.ShapeDtypeStruct((1, 1), f32),
            jax.ShapeDtypeStruct((64, COLS), f32),
            jax.ShapeDtypeStruct((1, COLS), f32),
            jax.ShapeDtypeStruct((A, COLS), f32),
            jax.ShapeDtypeStruct((1, COLS), f32),
        ),
        in_specs=[vmem] * 4,
        out_specs=(vmem,) * 6,
        name="write_outputs",
    )(*step_out)
    return (
        adv.T,
        mean.reshape(1),
        grad_w,
        grad_gain.reshape(COLS),
        grad_policy.T,
        grad_value.reshape(COLS),
    )


def solution(mesh):
    placed = (
        P(("role", "dp"), None, "mp"),
        P(("role", "dp"), None, "mp"),
        P("dp", "mp"),
        P("mp"),
        P("mp", None),
        P("mp"),
        P(("role", "dp"), None),
        P(("role", "dp"), None),
        P(("role", "dp"), None),
        P(("role", "dp")),
        P(("role", "dp")),
    )
    return jax.shard_map(
        per_device,
        mesh=mesh,
        in_specs=placed,
        out_specs=(
            P(("role", "dp"), None),
            P("dp"),
            P("dp", "mp"),
            P("mp"),
            P("mp", None),
            P("mp"),
        ),
        check_vma=False,
    )
```

```python
import jax
import jax.numpy as jnp
from jax import lax
from jax.experimental import pallas as pl
from jax.experimental.pallas import tpu as pltpu
from jax.sharding import PartitionSpec as P

D = 2048
A = 43
STEPS = 8
ROWS = 256
COLS = 512
HALF = 256
HP = 64
RAW = 48

discount = 0.99
trace_decay = 0.95
value_weight = 0.5
epsilon = 1e-05

MESH = pl.DeviceIdType.MESH
bf16 = jnp.bfloat16
f32 = jnp.float32
i32 = jnp.int32

NN = (((1,), (0,)), ((), ()))
NT = (((1,), (1,)), ((), ()))
TN = (((0,), (0,)), ((), ()))


def mul(a, b, dims):
    return lax.dot_general(a, b, dims, preferred_element_type=f32)


def parts_of(a, n):
    out = []
    for _ in range(n):
        high = a.astype(bf16)
        out.append(high)
        a = a - high.astype(f32)
    return out


FAR_FIRST = (4, 3, 5, 2, 6, 1, 7)


def kernel(
    resid_h, ctx_h, w_h, gain_h, policy_h, value_h,
    rewards_h, resets_h, actions_h, lengths_h, assign_h,
    adv_out, misc_out, gw_out, heads_out,
    resid, gain, policy, value, rewards, resets, actions, lengths, assign,
    ctxbuf, ctx_t, wbuf, psend, precv, stream_s, gstream,
    rawbuf, l1, l2, lsrc, heads_t, qsrc, qmate, qsum, q1, q2, qf,
    pb, ra, rb, sa2, sb2, ra2, rb2,
    s_all, r_in, r_ctx, r_w, r_wy, r_p, r_raw, r_l1, r_l2, r_g,
    r_q0, r_q1, r_q2, r_q3, r_q4, r_ra, r_rb, r_ra2, r_rb2, r_f, tokens,
):
    role = lax.axis_index("role")
    dp = lax.axis_index("dp")
    x = lax.axis_index("mp")
    z = dp // 4
    h = (dp // 2) % 2
    c = dp % 2
    y = h * 4 + role
    r = role
    o = 1 - c
    me16 = z * 2 + c

    def dev(dx, dy, dz, core):
        yy = (y + dy + 8) % 8
        return {
            "role": yy % 4,
            "dp": ((z + dz + 8) % 8) * 4 + (yy // 4) * 2 + core,
            "mp": (x + dx + 4) % 4,
        }

    mate = dev(0, 0, 0, o)
    pending = []

    def remote(src, dst, rsem, device):
        slot = len(pending)
        return pltpu.make_async_remote_copy(
            src_ref=src,
            dst_ref=dst,
            send_sem=s_all.at[slot],
            recv_sem=rsem,
            device_id=device,
            device_id_type=MESH,
        )

    def send(src, dst, rsem, device):
        copy = remote(src, dst, rsem, device)
        copy.start()
        pending.append((None, copy))

    def send_when(condition, src, dst, rsem, device):
        copy = remote(src, dst, rsem, device)
        pl.when(condition)(copy.start)
        pending.append((condition, copy))

    def send_or_keep(here, src, dst, rsem, device):
        copy = remote(src, dst, rsem, device)
        away = jnp.logical_not(here)

        @pl.when(here)
        def _():
            pltpu.make_async_copy(src, dst, rsem).start()

        @pl.when(away)
        def _():
            copy.start()

        pending.append((away, copy))

    def arrived(dst, rsem):
        pltpu.make_async_copy(dst, dst, rsem).wait()

    small = [
        (gain_h, gain), (policy_h, policy), (value_h, value), (rewards_h, rewards),
        (resets_h, resets), (actions_h, actions), (lengths_h, lengths), (assign_h, assign),
        (resid_h, resid),
    ]
    for n, (src, dst) in enumerate(small):
        pltpu.make_async_copy(src, dst, r_in.at[n]).start()

    barrier = pltpu.get_barrier_semaphore()
    peers = [mate, dev(1, 0, 0, 0), dev(1, 0, 0, 1), dev(3, 0, 0, 0), dev(3, 0, 0, 1)]
    peers += [dev(0, 0, d, c) for d in (1, 2, 6, 7)]
    peers += [dev(0, 1, 0, c), dev(0, 7, 0, c)]
    source = 3 * (1 - r // 2)
    peers += [{"role": source, "dp": z * 4 + (1 - h) * 2 + core, "mp": x} for core in range(2)]
    border = r % 3 == 0
    for peer in peers:
        pl.semaphore_signal(barrier, inc=1, device_id=peer, device_id_type=MESH)
    pl.semaphore_wait(barrier, len(peers) - 2 + jnp.where(border, 4, 0))

    def tell(n):
        pl.semaphore_signal(tokens.at[2 * n], inc=1, device_id=dev(0, 1, 0, c), device_id_type=MESH)
        pl.semaphore_signal(
            tokens.at[2 * n + 1], inc=1, device_id=dev(0, 7, 0, c), device_id_type=MESH
        )

    def hear(n):
        pl.semaphore_wait(tokens.at[2 * n], 1)
        pl.semaphore_wait(tokens.at[2 * n + 1], 1)

    tell(0)

    mine = pl.ds(pl.multiple_of((y % 2) * HALF, HALF), HALF)
    theirs = pl.ds(pl.multiple_of((1 - y % 2) * HALF, HALF), HALF)
    for n in range(2):
        to_role = jnp.where(r == 3, n, 3 - n)
        cols = pl.ds(pl.multiple_of((to_role % 2) * HALF, HALF), HALF)
        across = {"role": to_role, "dp": z * 4 + (1 - h) * 2 + h, "mp": x}
        send_when(
            border, w_h.at[:, :, cols], wbuf.at[z, c, :, :, cols], r_w.at[z * 2 + c], across
        )
    send_or_keep(
        c == h, w_h.at[:, :, mine], wbuf.at[z, c, :, :, mine], r_w.at[z * 2 + c], mate
    )

    def piece(zz, core):
        return ctx_h.at[:, pl.ds(pl.multiple_of(zz * 256 + core * 128, 128), 128)]

    def ctx_sem(m, cc, zz):
        return r_ctx.at[(m * 2 + cc) * 2 + zz]

    for first in range(2):
        for dx, zz in ((1, first), (3, 1 - first)):
            for core in range(2):
                send(piece(zz, core), ctxbuf.at[x, c, zz], ctx_sem(x, c, zz), dev(dx, 0, 0, core))
    for zz in range(2):
        pltpu.make_async_copy(piece(zz, c), ctxbuf.at[x, c, zz], ctx_sem(x, c, zz)).start()
        send(piece(zz, o), ctxbuf.at[x, c, zz], ctx_sem(x, c, zz), mate)

    def w_block(zz, cc):
        return wbuf.at[zz, cc, :, :, mine], r_w.at[zz * 2 + cc]

    def to_y(zz, cc):
        block = wbuf.at[zz, cc, :, :, mine]
        send(block, block, r_wy.at[zz * 2 + cc], dev(0, 1 if cc == 0 else 7, 0, c))

    for cc in range(2):
        block, sem = w_block(z, cc)
        arrived(block, sem)
        for d in (2, 6, 1, 7):
            send(block, block, sem, dev(0, 0, d, c))
        to_y(z, cc)

    for n in range(9):
        pltpu.make_async_copy(small[n][0], small[n][1], r_in.at[n]).wait()
    lane8 = lax.broadcasted_iota(i32, (8, ROWS), 1)
    sub8 = lax.broadcasted_iota(i32, (8, ROWS), 0)
    step = lane8 % STEPS
    own_step = step == sub8
    lane32 = lax.broadcasted_iota(i32, (32, ROWS), 1)
    sub32 = lax.broadcasted_iota(i32, (32, ROWS), 0)
    env_b = (lane32 // STEPS == sub32).astype(f32).astype(bf16)

    def to_row(grid):
        wide = jnp.where(own_step, mul(grid.astype(f32).astype(bf16), env_b, NN), 0.0)
        return jnp.broadcast_to(jnp.sum(wide, axis=0, keepdims=True), (8, ROWS))

    def env_row(vector):
        return mul(jnp.broadcast_to(vector.astype(f32), (8, 32)).astype(bf16), env_b, NN)

    reward = to_row(rewards[...])
    keep = 1.0 - to_row(resets[...])
    action = to_row(actions[...])
    length = env_row(lengths[...])
    learner = env_row(assign[...])
    valid = (step.astype(f32) < length).astype(f32)
    learner_hit = jnp.broadcast_to(learner[0:1], (32, ROWS)) == sub32.astype(f32)
    head_rows = lax.broadcasted_iota(i32, (HP, COLS), 0)
    heads_t[...] = jnp.where(
        head_rows == A,
        jnp.broadcast_to(value[...].astype(f32).reshape(1, COLS), (HP, COLS)),
        jnp.concatenate([policy[...].astype(f32), jnp.zeros((HP - A, COLS), f32)], axis=0),
    ).astype(bf16)

    for m, zz, dx in (((x + 3) % 4, 0, 1), ((x + 1) % 4, 1, 3)):
        for cc in range(2):
            block = ctxbuf.at[m, cc, zz]
            arrived(block, ctx_sem(m, cc, zz))
            send(block, block, ctx_sem(m, cc, zz), dev(dx, 0, 0, c))

    hear(0)
    tell(1)
    for cc in range(2):
        for d in (6, 2):
            block, sem = w_block((z + d) % 8, cc)
            arrived(block, sem)
            if d == 6:
                if cc == 0:
                    send(block, block, sem, dev(0, 0, 2, c))
                send(block, block, sem, dev(0, 0, 1, c))
            else:
                if cc == 1:
                    send(block, block, sem, dev(0, 0, 6, c))
                send(block, block, sem, dev(0, 0, 7, c))
            to_y((z + d) % 8, cc)
    hear(1)
    tell(2)
    for d in (1, 7, 3, 5, 4):
        for cc in range(2):
            arrived(*w_block((z + d) % 8, cc))
            to_y((z + d) % 8, cc)

    for cc in range(2):
        for zz in range(2):
            arrived(ctxbuf.at[x, cc, zz], ctx_sem(x, cc, zz))
            m = (x + 2) % 4
            arrived(ctxbuf.at[m, cc, zz], ctx_sem(m, cc, zz))
        m = (x + 3) % 4
        arrived(ctxbuf.at[m, cc, 1], ctx_sem(m, cc, 1))
        m = (x + 1) % 4
        arrived(ctxbuf.at[m, cc, 0], ctx_sem(m, cc, 0))
    hear(2)
    for s in range(8):
        for cc in range(2):
            arrived(wbuf.at[s, cc, :, :, theirs], r_wy.at[s * 2 + cc])

    def project(core):
        total = None
        for m in range(4):
            left = jnp.concatenate([ctxbuf[m, core, 0], ctxbuf[m, core, 1]], axis=1)
            term = mul(left, wbuf[2 * m : 2 * m + 2].reshape(256, COLS), NN)
            total = term if total is None else total + term
        return total

    psend[...] = project(o)
    send(psend, precv, r_p.at[0], mate)
    stream_s[...] = resid[...].astype(f32) + project(c)
    arrived(precv, r_p.at[0])
    stream = stream_s[...] + precv[...]
    stream_s[...] = stream

    gains = gain[...]
    raw = None
    for part in parts_of(stream * gains, 3):
        term = mul(heads_t[...], part, NT)
        raw = term if raw is None else raw + term
    square = None
    for part in parts_of(stream * stream, 3):
        term = mul(jnp.ones((16, COLS), bf16), part, NT)
        square = term if square is None else square + term
    raw_rows = lax.broadcasted_iota(i32, (RAW, ROWS), 0)
    rawbuf[x] = jnp.where(
        raw_rows == A + 1, jnp.broadcast_to(square[0:1], (RAW, ROWS)), raw[0:RAW]
    )
    for d in (2, 1, 3):
        send(rawbuf.at[x], rawbuf.at[x], r_raw.at[x], dev(d, 0, 0, c))
    for m in range(4):
        for zz in range(2):
            for cc in range(2):
                ctx_t[2 * m + zz, :, cc * ROWS : cc * ROWS + ROWS] = ctxbuf[m, cc, zz].T
    for d in (1, 3, 2):
        xx = (x + d) % 4
        arrived(rawbuf.at[xx], r_raw.at[xx])
    raw = ((rawbuf[0] + rawbuf[1]) + rawbuf[2]) + rawbuf[3]

    inverse = lax.rsqrt(jnp.broadcast_to(raw[A + 1 : A + 2], (8, ROWS)) / D + epsilon)
    out = raw * jnp.broadcast_to(inverse[0:1], (RAW, ROWS))
    values = jnp.broadcast_to(out[A : A + 1], (8, ROWS))

    def later(v, n):
        return pltpu.roll(v, ROWS - n, 1)

    last = step == STEPS - 1
    next_values = jnp.where(last, 0.0, later(values, 1))
    delta = reward + discount * keep * next_values - values
    adv = valid * delta
    factor = jnp.where(last, 0.0, valid * (discount * trace_decay) * keep)
    adv = adv + factor * later(adv, 1)
    factor = factor * later(factor, 1)
    adv = adv + factor * later(adv, 2)
    factor = factor * later(factor, 2)
    adv = adv + factor * later(adv, 4)

    adv32 = jnp.broadcast_to(adv[0:1], (32, ROWS))
    valid32 = jnp.broadcast_to(valid[0:1], (32, ROWS))
    sums = jnp.sum(jnp.where(learner_hit, adv32, 0.0), axis=1, keepdims=True)
    counts = jnp.sum(jnp.where(learner_hit, valid32, 0.0), axis=1, keepdims=True)
    lane128 = lax.broadcasted_iota(i32, (32, 128), 1)
    sub128 = lax.broadcasted_iota(i32, (32, 128), 0)
    at_sum = lane128 == sub128
    at_count = lane128 == sub128 + 32
    message = jnp.sum(
        jnp.where(at_sum, sums, 0.0) + jnp.where(at_count, counts, 0.0), axis=0, keepdims=True
    )
    l1[me16] = message
    lsrc[...] = message
    for d in FAR_FIRST:
        for core in range(2):
            send(lsrc, l1.at[me16], r_l1.at[me16], dev(0, 0, d, core))
    send(lsrc, l1.at[me16], r_l1.at[me16], mate)

    act_rows = raw_rows < A
    logits = jnp.where(act_rows, out, -1e30)
    top = jnp.max(logits, axis=0, keepdims=True)
    expo = jnp.where(act_rows, jnp.exp(logits - top), 0.0)
    prob = expo / jnp.sum(expo, axis=0, keepdims=True)
    chosen = raw_rows.astype(f32) == jnp.broadcast_to(action[0:1], (RAW, ROWS))
    score = prob - jnp.where(chosen, 1.0, 0.0)
    adv_grid = None
    for part in parts_of(jnp.where(own_step, adv, 0.0), 3):
        term = mul(part, env_b, NT)
        adv_grid = term if adv_grid is None else adv_grid + term
    adv_out[...] = adv_grid

    for s in range(1, 16):
        ss = (me16 + s) % 16
        arrived(l1.at[ss], r_l1.at[ss])
    total = l1[0]
    for s in range(1, 16):
        total = total + l1[s]
    l2[y] = total
    for d in FAR_FIRST:
        send(l2.at[y], l2.at[y], r_l2.at[y], dev(0, d, 0, c))
    for d in range(1, 8):
        yy = (y + d) % 8
        arrived(l2.at[yy], r_l2.at[yy])
    total = l2[0]
    for s in range(1, 8):
        total = total + l2[s]
    wide = jnp.broadcast_to(total, (32, 128))
    sums = jnp.sum(jnp.where(at_sum, wide, 0.0), axis=1, keepdims=True)
    counts = jnp.sum(jnp.where(at_count, wide, 0.0), axis=1, keepdims=True)
    means = sums / counts
    own = jnp.sum(jnp.where(sub128 == dp, means, 0.0), axis=0, keepdims=True)
    misc_out[...] = jnp.broadcast_to(own, (8, 128))

    mean_row = jnp.sum(jnp.where(learner_hit, means, 0.0), axis=0, keepdims=True)
    count_row = jnp.sum(jnp.where(learner_hit, counts, 0.0), axis=0, keepdims=True)
    weight = valid[0:1] / count_row
    centered = adv[0:1] - mean_row
    grad_value_row = -value_weight * weight * adv[0:1]
    grad_out = jnp.where(
        act_rows,
        (weight * centered) * score,
        jnp.where(raw_rows == A, jnp.broadcast_to(grad_value_row, (RAW, ROWS)), 0.0),
    )
    inner = jnp.sum(grad_out * raw, axis=0, keepdims=True)
    inv = inverse[0:1]
    coef = inv * inv * inv * inner / D
    scaled_out = grad_out * inv
    tall = jnp.concatenate([scaled_out, jnp.broadcast_to(coef, (HP - RAW, ROWS))], axis=0)
    tall_rows = lax.broadcasted_iota(i32, (HP, ROWS), 0)
    tall = jnp.where(tall_rows <= RAW, tall, 0.0)
    tall_parts = parts_of(tall, 2)

    one_row = (lax.broadcasted_iota(i32, (HP, 128), 0) == RAW).astype(f32).astype(bf16)
    grad_normed = mul(tall_parts[0], heads_t[...], TN) + mul(tall_parts[1], heads_t[...], TN)
    coef_col = mul(tall_parts[0], one_row, TN) + mul(tall_parts[1], one_row, TN)
    stream = stream_s[...]
    coef_wide = jnp.concatenate([coef_col] * 4, axis=1)
    gstream[c] = (gains * grad_normed - stream * coef_wide).astype(bf16)
    send(gstream.at[c], gstream.at[c], r_g.at[0], mate)

    high, low = parts_of(stream, 2)
    q = mul(tall_parts[0], high, NN) + mul(tall_parts[0], low, NN) + mul(tall_parts[1], high, NN)
    for p in range(16):
        qsrc[p % 2, p // 2] = q[
            (p % 4) * 16 : (p % 4) * 16 + 16, (p // 4) * 128 : (p // 4) * 128 + 128
        ]
    send(qsrc.at[o], qmate, r_q0.at[0], mate)

    arrived(qmate, r_q0.at[0])
    qsum[...] = qsrc[c] + qmate[...]
    q1[z] = qsum[z]

    def filled(zz):
        return jnp.logical_or(c == 0, zz % 2 == 0)

    def arrived_when(condition, dst, rsem):
        @pl.when(condition)
        def _():
            arrived(dst, rsem)

    for d in FAR_FIRST:
        zz = (z + d) % 8
        send_when(filled(zz), qsum.at[zz], q1.at[z], r_q1.at[z], dev(0, 0, d, c))

    arrived(gstream.at[o], r_g.at[0])
    first_cols, last_cols = pl.ds(0, HALF), pl.ds(HALF, HALF)
    grads = gstream[...].reshape(2 * ROWS, COLS)
    for d in FAR_FIRST + (0,):
        zz = (z + d) % 8
        block = mul(ctx_t[zz], grads, NN).astype(bf16).reshape(2, 4, 16, COLS)
        pb[zz] = block
        if d:
            send(pb.at[zz, :, :, :, first_cols], ra.at[z], r_ra.at[z], dev(0, 0, d, c))
        else:
            ra[z] = block[:, :, :, 0:HALF]

    def gather_sum(buf, sems, own, wait_own):
        if wait_own:
            arrived(buf.at[own], sems.at[own])
        total = buf[own].astype(f32)
        for d in (1, 7, 2, 6, 3, 5, 4):
            n = (own + d) % 8
            arrived(buf.at[n], sems.at[n])
            total = total + buf[n].astype(f32)
        return total

    def to_half(block_of, dst, rsem):
        for n in (2, 1, 3, 0):
            rr = (r + n) % 4
            for core in range(2):
                block = block_of(core, rr)
                device = {"role": rr, "dp": z * 4 + c * 2 + core, "mp": x}
                if n:
                    send(block, dst, rsem, device)
                else:
                    here = jnp.logical_and(h == c, c == core)
                    send_or_keep(here, block, dst, rsem, device)

    to_half(lambda core, rr: pb.at[:, core, rr, :, last_cols], rb.at[y], r_rb.at[y])

    for d in range(1, 8):
        zz = (z + d) % 8
        arrived_when(filled(z), q1.at[zz], r_q1.at[zz])
    total = q1[0]
    for s in range(1, 8):
        total = total + q1[s]
    q2[y] = total
    for d in FAR_FIRST:
        send_when(filled(z), q2.at[y], q2.at[y], r_q2.at[y], dev(0, d, 0, c))

    sa2[...] = gather_sum(ra, r_ra, z, False)
    to_half(lambda core, rr: sa2.at[core, rr], ra2.at[y], r_ra2.at[y])
    sb2[...] = gather_sum(rb, r_rb, y, True)
    rb2[z] = sb2[z]
    for d in FAR_FIRST:
        send(sb2.at[(z + d) % 8], rb2.at[z], r_rb2.at[z], dev(0, 0, d, c))

    for d in range(1, 8):
        yy = (y + d) % 8
        arrived_when(filled(z), q2.at[yy], r_q2.at[yy])
    total = q2[0]
    for s in range(1, 8):
        total = total + q2[s]
    qf[c, z] = total
    for d in FAR_FIRST:
        send_when(filled(z), qf.at[c, z], qf.at[c, z], r_q3.at[z], dev(0, 0, d, c))

    def to_roles(part, cols):
        for d in (2, 1, 3):
            device = {"role": (r + d) % 4, "dp": dp, "mp": x}
            block = gw_out.at[r, :, cols]
            send(block, block, r_f.at[part * 4 + r], device)

    gw_out[r, :, 0:HALF] = gather_sum(ra2, r_ra2, y, True)
    to_roles(0, first_cols)
    gw_out[r, :, HALF:] = gather_sum(rb2, r_rb2, z, False)
    to_roles(1, last_cols)

    for d in range(1, 8):
        zz = (z + d) % 8
        arrived_when(filled(zz), qf.at[c, zz], r_q3.at[zz])
    send(qf.at[c], qf.at[c], r_q4.at[0], mate)
    arrived(qf.at[o], r_q4.at[0])
    rows = lax.broadcasted_iota(i32, (RAW, 128), 0)
    for lane in range(4):
        cols = slice(lane * 128, lane * 128 + 128)
        block = jnp.concatenate([qf[s % 2, lane * 2 + s // 2] for s in range(3)], axis=0)
        gain_row = jnp.sum(block * heads_t[0:RAW, cols].astype(f32), axis=0, keepdims=True)
        heads_out[:, cols] = jnp.where(
            rows == A + 1, jnp.broadcast_to(gain_row, (RAW, 128)), block * gains[:, cols]
        )

    for d in range(1, 4):
        rr = (r + d) % 4
        arrived(gw_out.at[rr, :, first_cols], r_f.at[rr])
        arrived(gw_out.at[rr, :, last_cols], r_f.at[4 + rr])

    for condition, copy in pending:
        if condition is None:
            copy.wait_send()
        else:
            pl.when(condition)(copy.wait_send)


def finish(adv, misc, gw, heads, adv_o, mean_o, gw_o, gain_o, policy_o, value_o):
    adv_o[...] = adv[...]
    mean_o[...] = misc[0:1, 0:1]
    gw_o[...] = gw[...].reshape(64, COLS)
    gain_o[...] = heads[A + 1 : A + 2]
    policy_o[...] = heads[0:A]
    value_o[...] = heads[A : A + 1]


def per_device(
    residual_in,
    context,
    w_out,
    norm_gain,
    policy_head,
    value_head,
    rewards,
    resets,
    actions,
    lengths,
    assignment,
):
    vmem = pl.BlockSpec(memory_space=pltpu.VMEM)
    hbm = pl.BlockSpec(memory_space=pltpu.HBM)
    dma = pltpu.SemaphoreType.DMA
    buffers = [
        pltpu.VMEM((ROWS, COLS), bf16),
        pltpu.VMEM((1, COLS), f32),
        pltpu.VMEM((A, COLS), bf16),
        pltpu.VMEM((COLS,), bf16),
        pltpu.VMEM((STEPS, 32), bf16),
        pltpu.VMEM((STEPS, 32), i32),
        pltpu.VMEM((STEPS, 32), i32),
        pltpu.VMEM((1, 32), i32),
        pltpu.VMEM((1, 32), i32),
        pltpu.VMEM((4, 2, 2, ROWS, 128), bf16),
        pltpu.VMEM((8, 128, 2 * ROWS), bf16),
        pltpu.VMEM((8, 2, 4, 16, COLS), bf16),
        pltpu.VMEM((ROWS, COLS), f32),
        pltpu.VMEM((ROWS, COLS), f32),
        pltpu.VMEM((ROWS, COLS), f32),
        pltpu.VMEM((2, ROWS, COLS), bf16),
        pltpu.VMEM((4, RAW, ROWS), f32),
        pltpu.VMEM((16, 1, 128), f32),
        pltpu.VMEM((8, 1, 128), f32),
        pltpu.VMEM((1, 128), f32),
        pltpu.VMEM((HP, COLS), bf16),
        pltpu.VMEM((2, 8, 16, 128), f32),
        pltpu.VMEM((8, 16, 128), f32),
        pltpu.VMEM((8, 16, 128), f32),
        pltpu.VMEM((8, 16, 128), f32),
        pltpu.VMEM((8, 16, 128), f32),
        pltpu.VMEM((2, 8, 16, 128), f32),
        pltpu.VMEM((8, 2, 4, 16, COLS), bf16),
        pltpu.VMEM((8, 2, 4, 16, HALF), bf16),
        pltpu.VMEM((8, 8, 16, HALF), bf16),
        pltpu.VMEM((2, 4, 16, HALF), f32),
        pltpu.VMEM((8, 16, HALF), f32),
        pltpu.VMEM((8, 16, HALF), f32),
        pltpu.VMEM((8, 16, HALF), f32),
    ]
    counts = [160, 9, 16, 16, 16, 1, 4, 16, 8, 1, 1, 8, 8, 8, 1, 8, 8, 8, 8, 8]
    step_out = pl.pallas_call(
        kernel,
        out_shape=(
            jax.ShapeDtypeStruct((STEPS, 32), f32),
            jax.ShapeDtypeStruct((8, 128), f32),
            jax.ShapeDtypeStruct((4, 16, COLS), f32),
            jax.ShapeDtypeStruct((RAW, COLS), f32),
        ),
        in_specs=[hbm] * 11,
        out_specs=(vmem,) * 4,
        scratch_shapes=buffers
        + [dma((n,)) for n in counts]
        + [pltpu.SemaphoreType.REGULAR((6,))],
        compiler_params=pltpu.CompilerParams(
            collective_id=0, has_side_effects=True, vmem_limit_bytes=62 * 1024 * 1024
        ),
        name="policy_step",
    )(
        residual_in.reshape(ROWS, COLS),
        context.reshape(ROWS, COLS),
        w_out.reshape(4, 16, COLS),
        norm_gain.reshape(1, COLS),
        policy_head.T,
        value_head,
        rewards.T,
        resets.T,
        actions.T,
        lengths.reshape(1, 32),
        assignment.reshape(1, 32),
    )
    adv, mean, grad_w, grad_gain, grad_policy, grad_value = pl.pallas_call(
        finish,
        out_shape=(
            jax.ShapeDtypeStruct((STEPS, 32), f32),
            jax.ShapeDtypeStruct((1, 1), f32),
            jax.ShapeDtypeStruct((64, COLS), f32),
            jax.ShapeDtypeStruct((1, COLS), f32),
            jax.ShapeDtypeStruct((A, COLS), f32),
            jax.ShapeDtypeStruct((1, COLS), f32),
        ),
        in_specs=[vmem] * 4,
        out_specs=(vmem,) * 6,
        name="write_outputs",
    )(*step_out)
    return (
        adv.T,
        mean.reshape(1),
        grad_w,
        grad_gain.reshape(COLS),
        grad_policy.T,
        grad_value.reshape(COLS),
    )


def solution(mesh):
    placed = (
        P(("role", "dp"), None, "mp"),
        P(("role", "dp"), None, "mp"),
        P("dp", "mp"),
        P("mp"),
        P("mp", None),
        P("mp"),
        P(("role", "dp"), None),
        P(("role", "dp"), None),
        P(("role", "dp"), None),
        P(("role", "dp")),
        P(("role", "dp")),
    )
    return jax.shard_map(
        per_device,
        mesh=mesh,
        in_specs=placed,
        out_specs=(
            P(("role", "dp"), None),
            P("dp"),
            P("dp", "mp"),
            P("mp"),
            P("mp", None),
            P("mp"),
        ),
        check_vma=False,
    )
```
